256 devices in a mesh: row: 8 (over z), col: 32 (over x, y, core).
Axes of the slice: x: 4, y: 4, z: 8, core: 2. Of those that a mesh axis runs over, the one named last changes fastest.
Arguments:
- root_inv: bfloat16 [8192, 8192], P('row', 'col'), may hold values from -0.0625 to 0.0625
- panel: bfloat16 [8192, 4096], P(None, 'col'), may hold values from -1.5 to 1.5
- pattern: int32 [64, 32], replicated, may hold values 0 or 1
- child_diag: float32 [4096, 4096], P('row', 'col'), may hold values from -6 to 6
- owner: int32 [32], replicated, may hold values from 0 to 31, each once
Outputs:
- off_block: float32 [8192, 4096], P('row', 'col')
- diag_block: float32 [4096, 4096], P('row', 'col')
- owned_rows: bfloat16 [4096, 4096], P('col', 'row')
The draws below stay inside these ranges and needn't reach their ends.
Inputs may be any that keep to these rules, and one draw needn't show every extreme that they name: owner is a permutation of the 32 block columns.
All inputs are finite; a program needn't handle non-finite values.
Results may differ from the reference program's by a relative error of at most 0.0039.
Values may be sent and summed in bfloat16 or wider, within the bound.
A program may use at most 128 MiB of HBM per device.

```python
import jax
import jax.numpy as jnp

SEP = 8192
CHILD = 4096
BLK = 128
NBR = 64
NBC = 32


def plant(entries, stream_key, least, largest):
    longest = entries.shape.index(max(entries.shape))
    spots = []
    for shift in (0, 1):
        where = [jax.random.randint(jax.random.fold_in(stream_key, axis), (), 0, length) for axis, length in enumerate(entries.shape)]
        where[longest] = (where[longest] + shift) % entries.shape[longest]
        spots.append(tuple(where))
    return entries.at[spots[0]].set(least).at[spots[1]].set(largest)


def block_scale(own_key, extent, split, smallest, high):
    def one(position, shards_of):
        steps = jax.random.uniform(jax.random.fold_in(jax.random.fold_in(own_key, 6), position), (shards_of,), jnp.float32, smallest / len(split), high / len(split))
        return jnp.repeat(jnp.exp(steps), extent[position] // shards_of).reshape((-1,) + (1,) * (len(extent) - position - 1))

    level = one(*split[0])
    for cut in split[1:]:
        level = level * one(*cut)
    return level


def normal_values(key, dims, scale, limit, shards=(), dtype=jnp.bfloat16):
    array = jax.random.normal(key, dims, jnp.float32) * scale
    if len(shards) > 0:
        array = block_scale(key, dims, shards, -0.22, 0.18) * array
    return jnp.clip(array, min=-limit, max=limit).astype(dtype)


def setup_inputs(seed: int = 0) -> dict:
    seeds = jax.random.split(jax.random.key(seed), 6)
    return {
        "root_inv": normal_values(seeds[0], (SEP, SEP), SEP ** -0.5, 0.0625, ((0, 8), (1, 32))),
        "panel": normal_values(seeds[1], (SEP, CHILD), (1.0 / SEP ** 0.25), 1.5, ((1, 32),)),
        "pattern": plant((jax.random.randint(seeds[2], (NBR, NBC), 0, 2) < 1).astype(jnp.int32), jax.random.fold_in(seeds[2], 1), 0, 1),
        "child_diag": normal_values(seeds[3], (CHILD, CHILD), 0.5, 6.0, ((0, 8), (1, 32)), jnp.float32),
        "owner": jax.random.permutation(seeds[4], NBC).astype(jnp.int32),
    }


def reference(root_inv, panel, pattern, child_diag, owner):
    expanded = jnp.repeat(jnp.repeat(pattern, BLK, 0), BLK, 1)
    masked = jnp.where(expanded == 1, panel, jnp.zeros_like(panel))
    off_block = -jnp.dot(root_inv, masked, preferred_element_type=jnp.float32)
    off_wire = off_block.astype(jnp.bfloat16)
    diag_block = child_diag - jnp.dot(masked.T, off_wire, preferred_element_type=jnp.float32)
    diag_wire = diag_block.astype(jnp.bfloat16)
    columns = diag_wire.reshape(CHILD, NBC, BLK)
    taken = jnp.take(columns, owner.astype(jnp.int32), axis=1)
    owned_rows = taken.transpose(1, 2, 0).reshape(CHILD, CHILD)
    return off_block, diag_block, owned_rows
```

```python
import functools

import jax
import jax.numpy as jnp
from jax import lax
from jax.experimental import pallas as pl
from jax.experimental.pallas import tpu as pltpu
from jax.sharding import PartitionSpec as P

MESH = pl.DeviceIdType.MESH
BF = jnp.bfloat16
F32 = jnp.float32

NX, NY, NZ = 4, 4, 8
Z_STEPS = 2
DIRECT = (0, 3, 4, 5)


def at(start, size):
    return pl.ds(pl.multiple_of(start, size), size)


class Links:
    def __init__(self, send_sems, recv_sems):
        self.send_sems, self.recv_sems = send_sems, recv_sems
        self.count = 0
        self.started = []

    def send(self, src, dst, device):
        index = self.count
        self.count += 1
        copy = pltpu.make_async_remote_copy(
            src_ref=src,
            dst_ref=dst,
            send_sem=self.send_sems.at[index],
            recv_sem=self.recv_sems.at[index],
            device_id=device,
            device_id_type=MESH,
        )
        copy.start()
        self.started.append(copy)
        return copy

    def drain(self):
        for copy in self.started:
            copy.wait_send()


N_LINKS = 11 + 9 + 3 + 3 * len(DIRECT) + 2 * Z_STEPS + 48 + 32 + 12 + 7


def kernel(
    root, panel, pattern, child, owner,
    off_out, diag_out, own_out,
    r_all, panel_v, m_send, m_all, mr_all, child_all,
    prod, y_send, y_recv, o_all, d_all, z_send, z_recv, s_fin, e_all, w_all,
    sib_send, sib_recv, comb, x_send, x_recv,
    send_sems, recv_sems, e_recv, e_own_send, local_sems,
):
    z = lax.axis_index("row")
    c = lax.axis_index("col")
    h = c % 2
    y = (c // 2) % NY
    x = c // (2 * NY)

    def device(xx, yy, hh, zz):
        return (zz, (xx * NY + yy) * 2 + hh)

    def wrap(value, size):
        return (value + size) % size

    x_up, x_dn, x_far = wrap(x + 1, NX), wrap(x - 1, NX), wrap(x + 2, NX)
    y_up, y_dn, y_far = wrap(y + 1, NY), wrap(y - 1, NY), wrap(y + 2, NY)
    z_up, z_dn = wrap(z + 1, NZ), wrap(z - 1, NZ)
    z_pair = z + 1 - 2 * (z % 2)
    sib = device(x, y, 1 - h, z)
    to_xu, to_xd = device(x_up, y, h, z), device(x_dn, y, h, z)
    to_yu, to_yd = device(x, y_up, h, z), device(x, y_dn, h, z)
    to_zu, to_zd = device(x, y, h, z_up), device(x, y, h, z_dn)

    links = Links(send_sems, recv_sems)
    send = links.send

    seg_own = x * 2 + h
    own_r = pltpu.make_async_copy(root, r_all.at[seg_own], local_sems.at[0])
    own_r.start()
    own_panel = pltpu.make_async_copy(panel, panel_v, local_sems.at[1])
    own_panel.start()
    own_child = pltpu.make_async_copy(child, child_all.at[y], local_sems.at[2])
    own_child.start()

    barrier = pltpu.get_barrier_semaphore()
    peers = [sib, to_xu, to_xd, to_zu, to_zd]
    for k in range(1, NY):
        peers.append(device(x, wrap(y + k, NY), h, z))
        peers.append(device(x, wrap(y + k, NY), h, z_pair))
    for peer in peers:
        pl.semaphore_signal(barrier, inc=1, device_id=peer, device_id_type=MESH)
    pl.semaphore_wait(barrier, len(peers))

    top, low = pl.ds(0, 512), pl.ds(512, 512)
    r0 = send(root.at[top], r_all.at[seg_own, top], to_xu)
    r1 = send(root.at[low], r_all.at[seg_own, low], to_xd)
    r2 = send(root.at[low], r_all.at[seg_own, low], to_xu)
    r3 = send(root.at[top], r_all.at[seg_own, top], to_xd)
    r6 = send(root, r_all.at[seg_own], sib)

    own_panel.wait()

    def mask_into(dst_of, first_row, blocks):
        def body(i, carry):
            row = first_row + i * 128
            on = pattern[row // 128, c].astype(F32)
            value = panel_v[at(row, 128), :].astype(F32) * on
            dst_of(i, value)
            return carry

        lax.fori_loop(0, blocks, body, 0)

    def segment_row(s, yy):
        return (((s // 2) * NY + yy) * 2 + s % 2) * 256

    m_copies = {}
    for i, d in enumerate(DIRECT):
        s = (z + d) % NZ
        for k in range(1, NY):

            def put(b, value, i=i, k=k):
                m_send[i, k - 1, at(b * 128, 128), :] = value.astype(BF)

            mask_into(put, segment_row(s, (y + k) % NY), 2)
            m_copies[i, k] = send(
                m_send.at[i, k - 1],
                m_all.at[NY - k, at(s * 256, 256)],
                device(x, (y + k) % NY, h, z),
            )

    child_copies = [
        send(child, child_all.at[y], device(x, (y + k) % NY, h, z)) for k in range(1, NY)
    ]

    def own_segment(s, carry):
        def put(b, value):
            m_all[0, at(s * 256 + b * 128, 128), :] = value.astype(BF)

        mask_into(put, segment_row(s, y), 2)
        return carry

    lax.fori_loop(0, 8, own_segment, 0)

    def put_transposed(b, value):
        mr_all[at(seg_own * 128, 128), at(b * 128, 128)] = value.T.astype(BF)

    mask_into(put_transposed, z * 1024, 8)

    def m_slot(s):
        return m_all.at[pl.ds(1, NY - 1), at(s * 256, 256)]

    for k in range(1, NY):
        m_copies[0, k].wait_recv()
    up = send(m_slot(z), m_slot(z), to_zu)
    down = send(m_slot(z), m_slot(z), to_zd)

    r0.wait_recv()
    seg_dn, seg_up, seg_far = x_dn * 2 + h, x_up * 2 + h, x_far * 2 + h
    r4 = send(r_all.at[seg_dn, top], r_all.at[seg_dn, top], to_xu)
    r1.wait_recv()
    r5 = send(r_all.at[seg_up, low], r_all.at[seg_up, low], to_xd)

    for step in range(1, Z_STEPS):
        up.wait_recv()
        s = wrap(z - step, NZ)
        up = send(m_slot(s), m_slot(s), to_zu)
        down.wait_recv()
        s = wrap(z + step, NZ)
        down = send(m_slot(s), m_slot(s), to_zd)

    r2.wait_recv()
    r7 = send(r_all.at[seg_dn], r_all.at[seg_dn], sib)
    r3.wait_recv()
    r8 = send(r_all.at[seg_up], r_all.at[seg_up], sib)

    def mr_rows(s):
        return mr_all.at[at(s * 128, 128)]

    def mr_half(s, half):
        return mr_all.at[at(s * 128 + half * 64, 64)]

    t0 = send(mr_rows(seg_own), mr_rows(seg_own), to_xu)
    t1 = send(mr_rows(seg_own), mr_rows(seg_own), to_xd)
    t4 = send(mr_rows(seg_own), mr_rows(seg_own), sib)

    up.wait_recv()
    down.wait_recv()
    for i in range(1, len(DIRECT)):
        for k in range(1, NY):
            m_copies[i, k].wait_recv()
    own_r.wait()
    r6.wait_recv()
    r7.wait_recv()
    r8.wait_recv()

    def m_of(chunk, s):
        return m_all[(chunk - y + NY) % NY, at(s * 256, 256), :]

    def first_product(i, carry):
        chunk, rows = i // 4, at((i % 4) * 256, 256)
        total = None
        for xx in (x, x_dn, x_up):
            for hh in range(2):
                s = xx * 2 + hh
                term = jnp.dot(r_all[s, rows, :], m_of(chunk, s), preferred_element_type=F32)
                total = term if total is None else total + term
        prod[chunk, rows, :] = total
        return carry

    lax.fori_loop(0, 16, first_product, 0)

    r4.wait_recv()
    r9 = send(r_all.at[seg_far, top], r_all.at[seg_far, top], sib)
    r5.wait_recv()
    r10 = send(r_all.at[seg_far, low], r_all.at[seg_far, low], sib)

    t0.wait_recv()
    t2 = send(mr_half(seg_dn, 0), mr_half(seg_dn, 0), to_xu)
    t5 = send(mr_rows(seg_dn), mr_rows(seg_dn), sib)
    t1.wait_recv()
    t3 = send(mr_half(seg_up, 1), mr_half(seg_up, 1), to_xd)
    t6 = send(mr_rows(seg_up), mr_rows(seg_up), sib)

    r9.wait_recv()
    r10.wait_recv()

    ycopy, zcopy, ecopy = {}, {}, {}

    def finish(chunk, quarter):
        rows = at(quarter * 256, 256)
        total = prod[chunk, rows, :]
        for hh in range(2):
            s = x_far * 2 + hh
            total += jnp.dot(r_all[s, rows, :], m_of(chunk, s), preferred_element_type=F32)
        prod[chunk, rows, :] = total

    def half_rows(quarter, half):
        return at(quarter * 256 + half * 128, 128)

    def y_out(chunk, slot, value, to):
        y_send[chunk, slot] = value.astype(BF)
        ycopy[chunk, slot] = send(y_send.at[chunk, slot], y_recv.at[chunk, slot], to)

    def stage_a(chunk):
        finish(chunk, y_far)
        y_out(chunk, 0, prod[chunk, half_rows(y_far, 0), :], to_yu)
        y_out(chunk, 1, prod[chunk, half_rows(y_far, 1), :], to_yd)
        finish(chunk, y_up)
        y_out(chunk, 2, prod[chunk, half_rows(y_up, 1), :], to_yu)
        finish(chunk, y_dn)
        y_out(chunk, 3, prod[chunk, half_rows(y_dn, 0), :], to_yd)
        finish(chunk, y)

    def stage_b(chunk):
        ycopy[chunk, 0].wait_recv()
        value = prod[chunk, half_rows(y_up, 0), :] + y_recv[chunk, 0].astype(F32)
        y_out(chunk, 4, value, to_yu)
        ycopy[chunk, 1].wait_recv()
        value = prod[chunk, half_rows(y_dn, 1), :] + y_recv[chunk, 1].astype(F32)
        y_out(chunk, 5, value, to_yd)

    def o_copy(chunk, slot, quarter, half, to):
        ref = o_all.at[chunk, half_rows(quarter, half)]
        ycopy[chunk, slot] = send(ref, ref, to)

    def stage_c(chunk):
        ycopy[chunk, 3].wait_recv()
        ycopy[chunk, 4].wait_recv()
        o_all[chunk, half_rows(y, 0), :] = (
            prod[chunk, half_rows(y, 0), :] + y_recv[chunk, 3].astype(F32) + y_recv[chunk, 4].astype(F32)
        ).astype(BF)
        o_copy(chunk, 6, y, 0, to_yu)
        ycopy[chunk, 2].wait_recv()
        ycopy[chunk, 5].wait_recv()
        o_all[chunk, half_rows(y, 1), :] = (
            prod[chunk, half_rows(y, 1), :] + y_recv[chunk, 2].astype(F32) + y_recv[chunk, 5].astype(F32)
        ).astype(BF)
        o_copy(chunk, 7, y, 1, to_yd)
        o_copy(chunk, 8, y, 1, to_yu)
        o_copy(chunk, 9, y, 0, to_yd)

    def stage_d(chunk):
        ycopy[chunk, 6].wait_recv()
        o_copy(chunk, 10, y_dn, 0, to_yu)
        ycopy[chunk, 7].wait_recv()
        o_copy(chunk, 11, y_up, 1, to_yd)

    def z_out(chunk, slot, size, value, to):
        z_send[chunk, slot, pl.ds(0, size), :] = value
        zcopy[chunk, slot] = send(
            z_send.at[chunk, slot, pl.ds(0, size)], z_recv.at[chunk, slot, pl.ds(0, size)], to
        )

    def stage_e(chunk):
        for slot in (8, 9, 10, 11):
            ycopy[chunk, slot].wait_recv()

        def body(i, carry):
            rows = at(i * 256, 256)
            d_all[chunk, rows, :] = jnp.dot(mr_all[rows, :], o_all[chunk], preferred_element_type=F32)
            return carry

        lax.fori_loop(0, 4, body, 0)
        far = (z + 4) % NZ
        z_out(chunk, 0, 64, d_all[chunk, at(far * 128, 64), :], to_zu)
        z_out(chunk, 4, 64, d_all[chunk, at(far * 128 + 64, 64), :], to_zd)

    def stage_f(chunk, step):
        zcopy[chunk, step - 1].wait_recv()
        base = ((z + 4 - step) % NZ) * 128
        if step == 1:
            value = jnp.concatenate(
                [
                    d_all[chunk, at(base, 64), :] + z_recv[chunk, 0, pl.ds(0, 64), :],
                    d_all[chunk, at(base + 64, 64), :],
                ],
                axis=0,
            )
        else:
            value = d_all[chunk, at(base, 128), :] + z_recv[chunk, step - 1]
        z_out(chunk, step, 128, value, to_zu)
        zcopy[chunk, 4 + step - 1].wait_recv()
        base = ((z + 4 + step) % NZ) * 128
        if step == 1:
            value = jnp.concatenate(
                [
                    d_all[chunk, at(base, 64), :],
                    d_all[chunk, at(base + 64, 64), :] + z_recv[chunk, 4, pl.ds(0, 64), :],
                ],
                axis=0,
            )
        else:
            value = d_all[chunk, at(base, 128), :] + z_recv[chunk, 4 + step - 1]
        z_out(chunk, 4 + step, 128, value, to_zd)

    keeps = (z % 2) == (y // 2)
    e_z = 2 * (z // 2) + y // 2
    e_slot = 2 * (y % 2) + z % 2

    def e_dst(chunk):
        return e_all.at[chunk, at(e_slot * 128, 128)]

    def e_here(chunk):
        return pltpu.make_async_copy(s_fin.at[chunk], e_dst(chunk), e_recv.at[chunk, e_slot])

    def e_there(chunk):
        return pltpu.make_async_remote_copy(
            src_ref=s_fin.at[chunk],
            dst_ref=e_dst(chunk),
            send_sem=e_own_send.at[chunk, 0],
            recv_sem=e_recv.at[chunk, e_slot],
            device_id=device(x, y, h, z_pair),
            device_id_type=MESH,
        )

    def stage_g(chunk):
        zcopy[chunk, 3].wait_recv()
        zcopy[chunk, 7].wait_recv()
        s_fin[chunk] = (
            d_all[chunk, at(z * 128, 128), :] + z_recv[chunk, 3] + z_recv[chunk, 7]
        )
        for k in range(1, NY):
            copy = pltpu.make_async_remote_copy(
                src_ref=s_fin.at[chunk],
                dst_ref=e_dst(chunk),
                send_sem=e_own_send.at[chunk, k],
                recv_sem=e_recv.at[chunk, e_slot],
                device_id=device(x, (y + k) % NY, h, e_z),
                device_id_type=MESH,
            )
            copy.start()
            links.started.append(copy)

        @pl.when(keeps)
        def _():
            e_here(chunk).start()

        @pl.when(jnp.logical_not(keeps))
        def _():
            e_there(chunk).start()

    def stage_h(chunk):
        for slot in range(4):
            ref = e_all.at[chunk, pl.ds(slot * 128, 128)]
            pltpu.make_async_copy(ref, ref, e_recv.at[chunk, slot]).wait()
        w_all[chunk] = (child_all[chunk] + e_all[chunk]).astype(BF)

    t2_waited = False
    stages = [
        stage_a, stage_b, stage_c, stage_d, stage_e,
        lambda ch: stage_f(ch, 1), lambda ch: stage_f(ch, 2), lambda ch: stage_f(ch, 3),
        stage_g, stage_h,
    ]
    for step in range(len(stages) + NY - 1):
        if step == 3:
            t2.wait_recv()
            t3.wait_recv()
            t7 = send(mr_rows(seg_far), mr_rows(seg_far), sib)
            own_child.wait()
            for copy in child_copies:
                copy.wait_recv()
        if step == 4:
            for copy in (t4, t5, t6, t7):
                copy.wait_recv()
        for chunk in range(NY):
            stage = step - chunk
            if 0 <= stage < len(stages):
                stages[stage](chunk)

    off_out[...] = o_all[y]
    diag_out[...] = child_all[y] + e_all[y]

    def candidate(xx, hh):
        t = owner[(xx * NY + y) * 2 + hh]
        on = jnp.logical_and(t // (2 * NY) == x, t % 2 == h).astype(F32)
        return w_all[(t // 2) % NY].astype(F32) * on

    for xx in range(NX):
        sib_send[xx] = candidate(xx, 1 - h).astype(BF)
    sib_copy = send(sib_send, sib_recv, sib)
    for xx in range(NX):
        comb[xx] = candidate(xx, h)
    sib_copy.wait_recv()
    for xx in range(NX):
        comb[xx] = comb[xx] + sib_recv[xx].astype(F32)

    xcopy = {}

    def x_out(slot, value, to):
        x_send[slot] = value.astype(BF)
        xcopy[slot] = send(x_send.at[slot], x_recv.at[slot], to)

    first, second = pl.ds(0, 256), pl.ds(256, 256)
    x_out(0, comb[x_far, first, :], to_xu)
    x_out(1, comb[x_far, second, :], to_xd)
    x_out(2, comb[x_up, second, :], to_xu)
    x_out(3, comb[x_dn, first, :], to_xd)
    xcopy[0].wait_recv()
    x_out(4, comb[x_up, first, :] + x_recv[0].astype(F32), to_xu)
    xcopy[1].wait_recv()
    x_out(5, comb[x_dn, second, :] + x_recv[1].astype(F32), to_xd)
    for slot in (2, 3, 4, 5):
        xcopy[slot].wait_recv()
    own_out[first, :] = (comb[x, first, :] + x_recv[3].astype(F32) + x_recv[4].astype(F32)).astype(BF)
    own_out[second, :] = (comb[x, second, :] + x_recv[2].astype(F32) + x_recv[5].astype(F32)).astype(BF)

    links.drain()
    for chunk in range(NY):

        @pl.when(jnp.logical_not(keeps))
        def _(chunk=chunk):
            e_there(chunk).wait_send()


def on_device(root_inv, panel, pattern, child_diag, owner):
    vmem = pl.BlockSpec(memory_space=pltpu.VMEM)
    smem = pl.BlockSpec(memory_space=pltpu.SMEM)
    hbm = pl.BlockSpec(memory_space=pl.ANY)
    off, diag, own = pl.pallas_call(
        kernel,
        out_shape=(
            jax.ShapeDtypeStruct((1024, 128), BF),
            jax.ShapeDtypeStruct((512, 128), F32),
            jax.ShapeDtypeStruct((512, 128), BF),
        ),
        in_specs=[hbm, hbm, smem, hbm, smem],
        out_specs=(vmem, vmem, vmem),
        scratch_shapes=[
            pltpu.VMEM((8, 1024, 256), BF),
            pltpu.VMEM((8192, 128), BF),
            pltpu.VMEM((len(DIRECT), NY - 1, 256, 128), BF),
            pltpu.VMEM((NY, 2048, 128), BF),
            pltpu.VMEM((1024, 1024), BF),
            pltpu.VMEM((NY, 512, 128), F32),
            pltpu.VMEM((NY, 1024, 128), F32),
            pltpu.VMEM((NY, 6, 128, 128), BF),
            pltpu.VMEM((NY, 6, 128, 128), BF),
            pltpu.VMEM((NY, 1024, 128), BF),
            pltpu.VMEM((NY, 1024, 128), F32),
            pltpu.VMEM((NY, 8, 128, 128), F32),
            pltpu.VMEM((NY, 8, 128, 128), F32),
            pltpu.VMEM((NY, 128, 128), F32),
            pltpu.VMEM((NY, 512, 128), F32),
            pltpu.VMEM((NY, 512, 128), BF),
            pltpu.VMEM((NX, 512, 128), BF),
            pltpu.VMEM((NX, 512, 128), BF),
            pltpu.VMEM((NX, 512, 128), F32),
            pltpu.VMEM((6, 256, 128), BF),
            pltpu.VMEM((6, 256, 128), BF),
            pltpu.SemaphoreType.DMA((N_LINKS,)),
            pltpu.SemaphoreType.DMA((N_LINKS,)),
            pltpu.SemaphoreType.DMA((NY, 4)),
            pltpu.SemaphoreType.DMA((NY, 4)),
            pltpu.SemaphoreType.DMA((3,)),
        ],
        compiler_params=pltpu.CompilerParams(
            collective_id=0, has_side_effects=True, vmem_limit_bytes=48 * 1024 * 1024
        ),
    )(root_inv, panel, pattern, child_diag, owner)
    return -off.astype(F32), diag, own.T


def solution(mesh):
    placed = (P("row", "col"), P(None, "col"), P(), P("row", "col"), P())
    return jax.shard_map(
        on_device,
        mesh=mesh,
        in_specs=placed,
        out_specs=(P("row", "col"), P("row", "col"), P("col", "row")),
        check_vma=False,
    )
```

```python
import functools

import jax
import jax.numpy as jnp
from jax import lax
from jax.experimental import pallas as pl
from jax.experimental.pallas import tpu as pltpu
from jax.sharding import PartitionSpec as P

MESH = pl.DeviceIdType.MESH
BF = jnp.bfloat16
F32 = jnp.float32

NX, NY, NZ = 4, 4, 8
Z_STEPS = 2
DIRECT = (0, 3, 4, 5)


def at(start, size):
    return pl.ds(pl.multiple_of(start, size), size)


class Links:
    def __init__(self, send_sems, recv_sems):
        self.send_sems, self.recv_sems = send_sems, recv_sems
        self.count = 0
        self.started = []

    def send(self, src, dst, device):
        index = self.count
        self.count += 1
        copy = pltpu.make_async_remote_copy(
            src_ref=src,
            dst_ref=dst,
            send_sem=self.send_sems.at[index],
            recv_sem=self.recv_sems.at[index],
            device_id=device,
            device_id_type=MESH,
        )
        copy.start()
        self.started.append(copy)
        return copy

    def drain(self):
        for copy in self.started:
            copy.wait_send()


N_LINKS = 11 + 8 + 3 + 3 * len(DIRECT) + 4 * Z_STEPS + NY * (12 + 8 + 3 + 1) + 3


def kernel(
    root, panel, pattern, child, owner,
    off_out, diag_out, own_out,
    r_all, panel_v, m_send, m_all, mr_own, mr_all, child_v, child_all,
    prod, p_send, y_send, y_recv, o_all, d_all, z_send, z_recv, z_last_send, z_last_recv,
    d_send, d_here, w_all, x_send, x_recv,
    send_sems, recv_sems, swap_sems, d_send_sems, d_recv_sems, local_sems,
):
    z = lax.axis_index("row")
    c = lax.axis_index("col")
    h = c % 2
    y = (c // 2) % NY
    x = c // (2 * NY)

    def device(xx, yy, hh, zz):
        return (zz, (xx * NY + yy) * 2 + hh)

    def wrap(value, size):
        return (value + size) % size

    x_up, x_dn, x_far = wrap(x + 1, NX), wrap(x - 1, NX), wrap(x + 2, NX)
    y_up, y_dn, y_far = wrap(y + 1, NY), wrap(y - 1, NY), wrap(y + 2, NY)
    z_up, z_dn = wrap(z + 1, NZ), wrap(z - 1, NZ)
    sib = device(x, y, 1 - h, z)
    to_xu, to_xd = device(x_up, y, h, z), device(x_dn, y, h, z)
    to_yu, to_yd = device(x, y_up, h, z), device(x, y_dn, h, z)
    to_zu, to_zd = device(x, y, h, z_up), device(x, y, h, z_dn)

    links = Links(send_sems, recv_sems)
    send = links.send

    seg_own = x * 2 + h
    own_r = pltpu.make_async_copy(root, r_all.at[seg_own], local_sems.at[0])
    own_r.start()
    own_panel = pltpu.make_async_copy(panel, panel_v, local_sems.at[1])
    own_panel.start()
    own_child = pltpu.make_async_copy(child, child_v, local_sems.at[2])
    own_child.start()

    barrier = pltpu.get_barrier_semaphore()
    partner = device(x, y_far, 1 - h, z)
    peers = [sib, partner, to_xu, to_xd, device(x_far, y, h, z), to_zu, to_zd]
    peers += [device(x, (y + k) % NY, h, z) for k in range(1, NY)]
    for peer in peers:
        pl.semaphore_signal(barrier, inc=1, device_id=peer, device_id_type=MESH)
    pl.semaphore_wait(barrier, len(peers))

    top, low = pl.ds(0, 512), pl.ds(512, 512)
    r0 = send(root.at[top], r_all.at[seg_own, top], to_xu)
    r1 = send(root.at[low], r_all.at[seg_own, low], to_xd)
    r6 = send(root, r_all.at[seg_own], sib)

    own_panel.wait()

    def mask_into(dst_of, first_row, blocks):
        def body(i, carry):
            row = first_row + i * 128
            on = pattern[c, row // 128].astype(F32)
            value = panel_v[at(row, 128), :].astype(F32) * on
            dst_of(i, value)
            return carry

        lax.fori_loop(0, blocks, body, 0)

    def segment_row(s, yy):
        return (((s // 2) * NY + yy) * 2 + s % 2) * 256

    own_lanes, other_lanes = at((y % 2) * 128, 128), at(((y + 1) % 2) * 128, 128)
    m_copies = {}

    def over_y(i):
        s = (z + DIRECT[i]) % NZ
        for k in range(1, NY):

            def put(b, value):
                m_send[i, k - 1, at(b * 128, 128), :] = value.astype(BF)

            mask_into(put, segment_row(s, (y + k) % NY), 2)
            m_copies[i, k] = send(
                m_send.at[i, k - 1],
                m_all.at[y // 2, at(s * 256, 256), own_lanes],
                device(x, (y + k) % NY, h, z),
            )

    over_y(0)
    def own_segment(s, carry):
        def put(b, value):
            m_all[y // 2, at(s * 256 + b * 128, 128), own_lanes] = value.astype(BF)

        mask_into(put, segment_row(s, y), 2)
        return carry

    lax.fori_loop(0, 8, own_segment, 0)

    r2 = send(root.at[low], r_all.at[seg_own, low], to_xu)
    r3 = send(root.at[top], r_all.at[seg_own, top], to_xd)

    def put_transposed(b, value):
        mr_own[:, at(b * 128, 128)] = value.T.astype(BF)

    mask_into(put_transposed, z * 1024, 8)
    stays = h == y // 2

    def swap():
        return pltpu.make_async_remote_copy(
            src_ref=mr_own,
            dst_ref=mr_all.at[at((x * 2 + 1 - h) * 128, 128)],
            send_sem=swap_sems.at[0],
            recv_sem=swap_sems.at[1],
            device_id=partner,
            device_id_type=MESH,
        )

    @pl.when(stays)
    def _():
        pltpu.make_async_copy(mr_own, mr_all.at[at(seg_own * 128, 128)], swap_sems.at[1]).start()

    @pl.when(jnp.logical_not(stays))
    def _():
        swap().start()

    def slot_of(yy):
        return 2 * (yy % 2) + yy // 2

    def along_z(s, to):
        rows = at(s * 256, 256)
        refs = m_all.at[1 - y // 2, rows], m_all.at[y // 2, rows, other_lanes]
        return [send(ref, ref, to) for ref in refs]

    def arrived(copies):
        for copy in copies:
            copy.wait_recv()

    for k in range(1, NY):
        m_copies[0, k].wait_recv()
    up, down = along_z(z, to_zu), along_z(z, to_zd)
    for i in range(1, len(DIRECT)):
        over_y(i)
    own_child.wait()
    e_slot = slot_of(y)
    child_all[y] = child_v[at(e_slot * 128, 128), :]

    r0.wait_recv()
    seg_dn, seg_up, seg_far = x_dn * 2 + h, x_up * 2 + h, x_far * 2 + h
    r4 = send(r_all.at[seg_dn, top], r_all.at[seg_dn, top], to_xu)
    r1.wait_recv()
    r5 = send(r_all.at[seg_up, low], r_all.at[seg_up, low], to_xd)

    for step in range(1, Z_STEPS):
        arrived(up)
        up = along_z(wrap(z - step, NZ), to_zu)
        arrived(down)
        down = along_z(wrap(z + step, NZ), to_zd)

    r2.wait_recv()
    r7 = send(r_all.at[seg_dn], r_all.at[seg_dn], sib)
    r3.wait_recv()
    r8 = send(r_all.at[seg_up], r_all.at[seg_up], sib)

    def mr_rows(s):
        return mr_all.at[at(s * 128, 128)]

    def mr_half(s, half):
        return mr_all.at[at(s * 128 + half * 64, 64)]

    arrived(up)
    arrived(down)
    for i in range(1, len(DIRECT)):
        for k in range(1, NY):
            m_copies[i, k].wait_recv()
    child_copies = []
    for k in range(1, NY):
        yy = (y + k) % NY
        child_copies.append(
            send(child_v.at[at(slot_of(yy) * 128, 128)], child_all.at[y], device(x, yy, h, z))
        )
    own_r.wait()
    r6.wait_recv()
    r7.wait_recv()
    r8.wait_recv()

    def m_of(pair, s):
        return m_all[pair, at(s * 256, 256), :]

    def first_product(i, carry):
        pair, rows = i // 4, at((i % 4) * 256, 256)
        total = None
        for xx in (x, x_dn, x_up):
            for hh in range(2):
                s = xx * 2 + hh
                term = jnp.dot(r_all[s, rows, :], m_of(pair, s), preferred_element_type=F32)
                total = term if total is None else total + term
        prod[pair, rows, :] = total
        return carry

    lax.fori_loop(0, 4, first_product, 0)

    r4.wait_recv()
    r9 = send(r_all.at[seg_far, top], r_all.at[seg_far, top], sib)
    r5.wait_recv()
    r10 = send(r_all.at[seg_far, low], r_all.at[seg_far, low], sib)

    lax.fori_loop(4, 8, first_product, 0)
    pltpu.make_async_copy(mr_own, mr_rows(seg_own), swap_sems.at[1]).wait()
    t0 = send(mr_rows(seg_own), mr_rows(seg_own), to_xu)
    t1 = send(mr_rows(seg_own), mr_rows(seg_own), to_xd)
    t4 = send(mr_rows(seg_own), mr_rows(seg_own), sib)

    r9.wait_recv()
    r10.wait_recv()

    ycopy, zcopy = {}, {}

    def finish(pair):
        def body(quarter, carry):
            rows = at(quarter * 256, 256)
            total = prod[pair, rows, :]
            for hh in range(2):
                s = x_far * 2 + hh
                total += jnp.dot(r_all[s, rows, :], m_of(pair, s), preferred_element_type=F32)
            prod[pair, rows, :] = total
            p_send[2 * pair, rows, :] = total[:, :128].astype(BF)
            p_send[2 * pair + 1, rows, :] = total[:, 128:].astype(BF)
            return carry

        lax.fori_loop(0, 4, body, 0)

    def part(chunk, rows):
        return prod[chunk // 2, rows, pl.ds((chunk % 2) * 128, 128)]

    def half_rows(quarter, half):
        return at(quarter * 256 + half * 128, 128)

    def y_out(chunk, slot, value, to):
        y_send[chunk, slot - 4] = value.astype(BF)
        ycopy[chunk, slot] = send(y_send.at[chunk, slot - 4], y_recv.at[chunk, slot], to)

    def p_out(chunk, slot, quarter, half, to):
        ycopy[chunk, slot] = send(
            p_send.at[chunk, half_rows(quarter, half)], y_recv.at[chunk, slot], to
        )

    def stage_a(chunk):
        if chunk % 2 == 0:
            finish(chunk // 2)
        p_out(chunk, 0, y_far, 0, to_yu)
        p_out(chunk, 1, y_far, 1, to_yd)
        p_out(chunk, 2, y_up, 1, to_yu)
        p_out(chunk, 3, y_dn, 0, to_yd)

    def stage_b(chunk):
        ycopy[chunk, 0].wait_recv()
        value = part(chunk, half_rows(y_up, 0)) + y_recv[chunk, 0].astype(F32)
        y_out(chunk, 4, value, to_yu)
        ycopy[chunk, 1].wait_recv()
        value = part(chunk, half_rows(y_dn, 1)) + y_recv[chunk, 1].astype(F32)
        y_out(chunk, 5, value, to_yd)

    def o_copy(chunk, slot, quarter, half, to):
        ref = o_all.at[chunk, half_rows(quarter, half)]
        ycopy[chunk, slot] = send(ref, ref, to)

    def stage_c(chunk):
        ycopy[chunk, 3].wait_recv()
        ycopy[chunk, 4].wait_recv()
        o_all[chunk, half_rows(y, 0), :] = (
            part(chunk, half_rows(y, 0)) + y_recv[chunk, 3].astype(F32) + y_recv[chunk, 4].astype(F32)
        ).astype(BF)
        o_copy(chunk, 6, y, 0, to_yu)
        ycopy[chunk, 2].wait_recv()
        ycopy[chunk, 5].wait_recv()
        o_all[chunk, half_rows(y, 1), :] = (
            part(chunk, half_rows(y, 1)) + y_recv[chunk, 2].astype(F32) + y_recv[chunk, 5].astype(F32)
        ).astype(BF)
        o_copy(chunk, 7, y, 1, to_yd)
        o_copy(chunk, 8, y, 1, to_yu)
        o_copy(chunk, 9, y, 0, to_yd)

    def stage_d(chunk):
        ycopy[chunk, 6].wait_recv()
        o_copy(chunk, 10, y_dn, 0, to_yu)
        ycopy[chunk, 7].wait_recv()
        o_copy(chunk, 11, y_up, 1, to_yd)

    def z_out(chunk, slot, size, value, to):
        if slot % 4 == 3:
            src, dst = z_last_send.at[chunk, slot // 4], z_last_recv.at[chunk, slot // 4]
            src[...] = value
        else:
            part = pl.ds(0, size)
            src, dst = z_send.at[chunk, slot, part], z_recv.at[chunk, slot, part]
            src[...] = value.astype(BF)
        zcopy[chunk, slot] = send(src, dst, to)

    def stage_e(chunk):
        for slot in (8, 9, 10, 11):
            ycopy[chunk, slot].wait_recv()

        def body(i, carry):
            rows = at(i * 512, 512)
            d_all[chunk, rows, :] = jnp.dot(mr_all[rows, :], o_all[chunk], preferred_element_type=F32)
            return carry

        lax.fori_loop(0, 2, body, 0)
        far = ((z + 4) % NZ) * 128
        z_out(chunk, 0, 64, d_all[chunk, at(far, 64), :], to_zu)
        z_out(chunk, 4, 64, d_all[chunk, at(far + 64, 64), :], to_zd)

    def stage_f(chunk, step):
        for slot, ahead, to in ((step, 4 - step, to_zu), (4 + step, 4 + step, to_zd)):
            zcopy[chunk, slot - 1].wait_recv()
            base = ((z + ahead) % NZ) * 128
            if step == 1:
                halves = [d_all[chunk, at(base, 64), :], d_all[chunk, at(base + 64, 64), :]]
                halves[slot // 4] += z_recv[chunk, slot - 1, pl.ds(0, 64), :].astype(F32)
                value = jnp.concatenate(halves, axis=0)
            else:
                value = d_all[chunk, at(base, 128), :] + z_recv[chunk, slot - 1].astype(F32)
            z_out(chunk, slot, 128, value, to)

    e_copies, w_copies = {}, []

    def d_there(chunk):
        return pltpu.make_async_remote_copy(
            src_ref=d_send.at[chunk],
            dst_ref=d_here.at[at(e_slot * 128, 128)],
            send_sem=d_send_sems.at[chunk],
            recv_sem=d_recv_sems.at[e_slot],
            device_id=device(x, chunk, h, z),
            device_id_type=MESH,
        )

    def stage_g(chunk):
        zcopy[chunk, 3].wait_recv()
        zcopy[chunk, 7].wait_recv()
        value = d_all[chunk, at(z * 128, 128), :] + z_last_recv[chunk, 0] + z_last_recv[chunk, 1]
        value += child_all[chunk]
        ref = w_all.at[h, chunk, at(e_slot * 128, 128)]
        ref[...] = value.astype(BF)
        for k in (2, 1, 3):
            e_copies[chunk, k] = send(ref, ref, device(x, (y + k) % NY, h, z))
        d_send[chunk] = value

        @pl.when(y == chunk)
        def _():
            here = d_here.at[at(e_slot * 128, 128)]
            pltpu.make_async_copy(d_send.at[chunk], here, d_recv_sems.at[e_slot]).start()

        @pl.when(y != chunk)
        def _():
            d_there(chunk).start()

    def stage_h(chunk):
        for k in (1, 3, 2):
            e_copies[chunk, k].wait_recv()
        w_copies.append(send(w_all.at[h, chunk], w_all.at[h, chunk], sib))

    stages = [stage_a, stage_b, stage_c, stage_d, stage_e]
    stages += [functools.partial(stage_f, step=step) for step in (1, 2, 3)]
    stages += [stage_g, stage_h]
    for step in range(len(stages) + NY - 1):
        order = [chunk for chunk in range(NY) if 0 <= step - chunk < len(stages)]
        if step == 2:
            t0.wait_recv()
            t2 = send(mr_half(seg_dn, 0), mr_half(seg_dn, 0), to_xu)
            t5 = send(mr_rows(seg_dn), mr_rows(seg_dn), sib)
            t1.wait_recv()
            t3 = send(mr_half(seg_up, 1), mr_half(seg_up, 1), to_xd)
            t6 = send(mr_rows(seg_up), mr_rows(seg_up), sib)
        if step == 8:
            for copy in child_copies:
                copy.wait_recv()
        if step == 4:
            t2.wait_recv()
            t3.wait_recv()
            t7 = send(mr_rows(seg_far), mr_rows(seg_far), sib)
            order = [k for k in (1, 2, 3, 0) if step - k < len(stages)]
        for chunk in order:
            if step == 4 and chunk == 0:
                for copy in (t4, t5, t6, t7):
                    copy.wait_recv()
            stages[step - chunk](chunk)

    def candidate(xx):
        t = owner[(xx * NY + y) * 2 + h]
        on = (t // (2 * NY) == x).astype(F32)
        return w_all[t % 2, (t // 2) % NY].astype(F32) * on

    for copy in w_copies:
        copy.wait_recv()
    x_copies = []
    for k in (2, 1, 3):
        xx = (x + k) % NX
        x_send[k] = candidate(xx).astype(BF)
        x_copies.append(send(x_send.at[k], x_recv.at[k], device(xx, y, h, z)))
    off_out[...] = o_all[y]
    for slot in range(4):
        ref = d_here.at[pl.ds(slot * 128, 128)]
        pltpu.make_async_copy(ref, ref, d_recv_sems.at[slot]).wait()
    diag_out[...] = d_here[...]
    own_out[...] = candidate(x).astype(BF)
    for copy in x_copies:
        copy.wait_recv()

    def add_up(i, carry):
        rows = at(i * 128, 128)
        total = own_out[rows, :].astype(F32)
        for k in (1, 2, 3):
            total += x_recv[k, rows, :].astype(F32)
        own_out[rows, :] = total.astype(BF)
        return carry

    lax.fori_loop(0, 4, add_up, 0)

    links.drain()
    for chunk in range(NY):

        @pl.when(y != chunk)
        def _(chunk=chunk):
            d_there(chunk).wait_send()

    @pl.when(jnp.logical_not(stays))
    def _():
        swap().wait_send()


def outputs(off, diag, own, off_out, diag_out, own_out):
    off_out[...] = -off[...].astype(F32)
    diag_out[...] = diag[...]
    for i in range(4):
        rows = pl.ds(i * 128, 128)
        own_out[:, rows] = own[rows, :].astype(F32).T.astype(BF)


def on_device(root_inv, panel, pattern, child_diag, owner):
    vmem = pl.BlockSpec(memory_space=pltpu.VMEM)
    smem = pl.BlockSpec(memory_space=pltpu.SMEM)
    hbm = pl.BlockSpec(memory_space=pl.ANY)
    off, diag, own = pl.pallas_call(
        kernel,
        out_shape=(
            jax.ShapeDtypeStruct((1024, 128), BF),
            jax.ShapeDtypeStruct((512, 128), F32),
            jax.ShapeDtypeStruct((512, 128), BF),
        ),
        in_specs=[hbm, hbm, smem, hbm, smem],
        out_specs=(vmem, vmem, vmem),
        scratch_shapes=[
            pltpu.VMEM((8, 1024, 256), BF),
            pltpu.VMEM((8192, 128), BF),
            pltpu.VMEM((len(DIRECT), NY - 1, 256, 128), BF),
            pltpu.VMEM((2, 2048, 256), BF),
            pltpu.VMEM((128, 1024), BF),
            pltpu.VMEM((1024, 1024), BF),
            pltpu.VMEM((512, 128), F32),
            pltpu.VMEM((NY, 128, 128), F32),
            pltpu.VMEM((2, 1024, 256), F32),
            pltpu.VMEM((NY, 1024, 128), BF),
            pltpu.VMEM((NY, 2, 128, 128), BF),
            pltpu.VMEM((NY, 6, 128, 128), BF),
            pltpu.VMEM((NY, 1024, 128), BF),
            pltpu.VMEM((NY, 1024, 128), F32),
            pltpu.VMEM((NY, 7, 128, 128), BF),
            pltpu.VMEM((NY, 7, 128, 128), BF),
            pltpu.VMEM((NY, 2, 128, 128), F32),
            pltpu.VMEM((NY, 2, 128, 128), F32),
            pltpu.VMEM((NY, 128, 128), F32),
            pltpu.VMEM((512, 128), F32),
            pltpu.VMEM((2, NY, 512, 128), BF),
            pltpu.VMEM((NX, 512, 128), BF),
            pltpu.VMEM((NX, 512, 128), BF),
            pltpu.SemaphoreType.DMA((N_LINKS,)),
            pltpu.SemaphoreType.DMA((N_LINKS,)),
            pltpu.SemaphoreType.DMA((2,)),
            pltpu.SemaphoreType.DMA((NY,)),
            pltpu.SemaphoreType.DMA((4,)),
            pltpu.SemaphoreType.DMA((3,)),
        ],
        compiler_params=pltpu.CompilerParams(
            collective_id=0, has_side_effects=True, vmem_limit_bytes=60 * 1024 * 1024
        ),
    )(root_inv, panel, pattern.T, child_diag, owner)
    return pl.pallas_call(
        outputs,
        out_shape=(
            jax.ShapeDtypeStruct((1024, 128), F32),
            jax.ShapeDtypeStruct((512, 128), F32),
            jax.ShapeDtypeStruct((128, 512), BF),
        ),
        in_specs=[vmem] * 3,
        out_specs=(vmem,) * 3,
        compiler_params=pltpu.CompilerParams(vmem_limit_bytes=60 * 1024 * 1024),
    )(off, diag, own)


def solution(mesh):
    placed = (P("row", "col"), P(None, "col"), P(), P("row", "col"), P())
    return jax.shard_map(
        on_device,
        mesh=mesh,
        in_specs=placed,
        out_specs=(P("row", "col"), P("row", "col"), P("col", "row")),
        check_vma=False,
    )
```

```python
import functools

import jax
import jax.numpy as jnp
from jax import lax
from jax.experimental import pallas as pl
from jax.experimental.pallas import tpu as pltpu
from jax.sharding import PartitionSpec as P

MESH = pl.DeviceIdType.MESH
BF = jnp.bfloat16
F32 = jnp.float32

NX, NY, NZ = 4, 4, 8
Z_STEPS = 2
DIRECT = (0, 3, 4, 5)


def at(start, size):
    return pl.ds(pl.multiple_of(start, size), size)


class Links:
    def __init__(self, send_sems, recv_sems):
        self.send_sems, self.recv_sems = send_sems, recv_sems
        self.count = 0
        self.started = []

    def send(self, src, dst, device):
        index = self.count
        self.count += 1
        copy = pltpu.make_async_remote_copy(
            src_ref=src,
            dst_ref=dst,
            send_sem=self.send_sems.at[index],
            recv_sem=self.recv_sems.at[index],
            device_id=device,
            device_id_type=MESH,
        )
        copy.start()
        self.started.append(copy)
        return copy

    def drain(self):
        for copy in self.started:
            copy.wait_send()


N_LINKS = 11 + 8 + 3 + 3 * len(DIRECT) + 4 * Z_STEPS + NY * (12 + 8 + 3 + 1) + 3


def kernel(
    root, panel, pattern, child, owner,
    off_out, diag_out, own_out,
    r_all, panel_v, m_send, m_all, mr_own, mr_all, child_v, child_all,
    prod, p_send, y_send, y_recv, o_all, d_all, z_send, z_recv, z_last_send, z_last_recv,
    d_send, d_here, w_all, last_send, own_all,
    send_sems, recv_sems, swap_sems, d_send_sems, d_recv_sems, local_sems,
):
    z = lax.axis_index("row")
    c = lax.axis_index("col")
    h = c % 2
    y = (c // 2) % NY
    x = c // (2 * NY)

    def device(xx, yy, hh, zz):
        return (zz, (xx * NY + yy) * 2 + hh)

    def wrap(value, size):
        return (value + size) % size

    x_up, x_dn, x_far = wrap(x + 1, NX), wrap(x - 1, NX), wrap(x + 2, NX)
    y_up, y_dn, y_far = wrap(y + 1, NY), wrap(y - 1, NY), wrap(y + 2, NY)
    z_up, z_dn = wrap(z + 1, NZ), wrap(z - 1, NZ)
    sib = device(x, y, 1 - h, z)
    to_xu, to_xd = device(x_up, y, h, z), device(x_dn, y, h, z)
    to_yu, to_yd = device(x, y_up, h, z), device(x, y_dn, h, z)
    to_zu, to_zd = device(x, y, h, z_up), device(x, y, h, z_dn)

    links = Links(send_sems, recv_sems)
    send = links.send

    seg_own = x * 2 + h
    own_r = pltpu.make_async_copy(root, r_all.at[seg_own], local_sems.at[0])
    own_r.start()
    own_panel = pltpu.make_async_copy(panel, panel_v, local_sems.at[1])
    own_panel.start()
    own_child = pltpu.make_async_copy(child, child_v, local_sems.at[2])
    own_child.start()

    barrier = pltpu.get_barrier_semaphore()
    partner = device(x, y_far, 1 - h, z)
    peers = [sib, partner, to_xu, to_xd, device(x_far, y, h, z), to_zu, to_zd]
    peers += [device(x, (y + k) % NY, h, z) for k in range(1, NY)]
    for peer in peers:
        pl.semaphore_signal(barrier, inc=1, device_id=peer, device_id_type=MESH)
    pl.semaphore_wait(barrier, len(peers))

    top, low = pl.ds(0, 512), pl.ds(512, 512)
    r0 = send(root.at[top], r_all.at[seg_own, top], to_xu)
    r1 = send(root.at[low], r_all.at[seg_own, low], to_xd)
    r6 = send(root, r_all.at[seg_own], sib)

    own_panel.wait()

    def mask_into(dst_of, first_row, blocks):
        def body(i, carry):
            row = first_row + i * 128
            on = pattern[c, row // 128].astype(F32)
            value = panel_v[at(row, 128), :].astype(F32) * on
            dst_of(i, value)
            return carry

        lax.fori_loop(0, blocks, body, 0)

    def segment_row(s, yy):
        return (((s // 2) * NY + yy) * 2 + s % 2) * 256

    own_lanes, other_lanes = at((y % 2) * 128, 128), at(((y + 1) % 2) * 128, 128)
    m_copies = {}

    def over_y(i):
        s = (z + DIRECT[i]) % NZ
        for k in range(1, NY):

            def put(b, value):
                m_send[i, k - 1, at(b * 128, 128), :] = value.astype(BF)

            mask_into(put, segment_row(s, (y + k) % NY), 2)
            m_copies[i, k] = send(
                m_send.at[i, k - 1],
                m_all.at[y // 2, at(s * 256, 256), own_lanes],
                device(x, (y + k) % NY, h, z),
            )

    over_y(0)
    def own_segment(s, carry):
        def put(b, value):
            m_all[y // 2, at(s * 256 + b * 128, 128), own_lanes] = value.astype(BF)

        mask_into(put, segment_row(s, y), 2)
        return carry

    lax.fori_loop(0, 8, own_segment, 0)

    r2 = send(root.at[low], r_all.at[seg_own, low], to_xu)
    r3 = send(root.at[top], r_all.at[seg_own, top], to_xd)

    def put_transposed(b, value):
        mr_own[:, at(b * 128, 128)] = value.T.astype(BF)

    mask_into(put_transposed, z * 1024, 8)
    stays = h == y // 2

    def swap():
        return pltpu.make_async_remote_copy(
            src_ref=mr_own,
            dst_ref=mr_all.at[at((x * 2 + 1 - h) * 128, 128)],
            send_sem=swap_sems.at[0],
            recv_sem=swap_sems.at[1],
            device_id=partner,
            device_id_type=MESH,
        )

    def slot_of(yy):
        return 2 * (yy % 2) + yy // 2

    def along_z(s, i, to):
        rows = at(s * 256, 256)
        ref = m_all.at[y // 2, rows, other_lanes] if i == 0 else m_all.at[1 - y // 2, rows]
        return send(ref, ref, to)

    def arrived(copies):
        for copy in copies:
            copy.wait_recv()

    for k in range(1, NY):
        m_copies[0, k].wait_recv()
    up, down = [], []
    for i in range(2):
        up.append(along_z(z, i, to_zu))
        down.append(along_z(z, i, to_zd))
    for i in range(1, len(DIRECT)):
        over_y(i)
    own_child.wait()
    e_slot = slot_of(y)
    child_all[y] = child_v[at(e_slot * 128, 128), :]

    r0.wait_recv()
    seg_dn, seg_up, seg_far = x_dn * 2 + h, x_up * 2 + h, x_far * 2 + h
    r4 = send(r_all.at[seg_dn, top], r_all.at[seg_dn, top], to_xu)
    r1.wait_recv()
    r5 = send(r_all.at[seg_up, low], r_all.at[seg_up, low], to_xd)

    for step in range(1, Z_STEPS):
        for i in range(2):
            up[i].wait_recv()
            up[i] = along_z(wrap(z - step, NZ), i, to_zu)
            down[i].wait_recv()
            down[i] = along_z(wrap(z + step, NZ), i, to_zd)

    r2.wait_recv()
    r7 = send(r_all.at[seg_dn], r_all.at[seg_dn], sib)
    r3.wait_recv()
    r8 = send(r_all.at[seg_up], r_all.at[seg_up], sib)

    def mr_rows(s):
        return mr_all.at[at(s * 128, 128)]

    def mr_half(s, half):
        return mr_all.at[at(s * 128 + half * 64, 64)]

    @pl.when(stays)
    def _():
        pltpu.make_async_copy(mr_own, mr_all.at[at(seg_own * 128, 128)], swap_sems.at[1]).start()

    @pl.when(jnp.logical_not(stays))
    def _():
        swap().start()

    arrived(up)
    arrived(down)
    for i in range(1, len(DIRECT)):
        for k in range(1, NY):
            m_copies[i, k].wait_recv()
    child_copies = []
    for k in range(1, NY):
        yy = (y + k) % NY
        child_copies.append(
            send(child_v.at[at(slot_of(yy) * 128, 128)], child_all.at[y], device(x, yy, h, z))
        )
    own_r.wait()
    r6.wait_recv()
    r7.wait_recv()
    r8.wait_recv()

    def m_of(pair, s):
        return m_all[pair, at(s * 256, 256), :]

    def first_product(i, carry):
        pair, rows = i // 4, at((i % 4) * 256, 256)
        total = None
        for xx in (x, x_dn, x_up):
            for hh in range(2):
                s = xx * 2 + hh
                term = jnp.dot(r_all[s, rows, :], m_of(pair, s), preferred_element_type=F32)
                total = term if total is None else total + term
        prod[pair, rows, :] = total
        return carry

    lax.fori_loop(0, 4, first_product, 0)

    r4.wait_recv()
    r9 = send(r_all.at[seg_far, top], r_all.at[seg_far, top], sib)
    r5.wait_recv()
    r10 = send(r_all.at[seg_far, low], r_all.at[seg_far, low], sib)

    lax.fori_loop(4, 8, first_product, 0)
    pltpu.make_async_copy(mr_own, mr_rows(seg_own), swap_sems.at[1]).wait()
    t0 = send(mr_rows(seg_own), mr_rows(seg_own), to_xu)
    t1 = send(mr_rows(seg_own), mr_rows(seg_own), to_xd)
    t4 = send(mr_rows(seg_own), mr_rows(seg_own), sib)

    r9.wait_recv()
    r10.wait_recv()

    ycopy, zcopy = {}, {}

    def finish(pair):
        def body(quarter, carry):
            rows = at(quarter * 256, 256)
            total = prod[pair, rows, :]
            for hh in range(2):
                s = x_far * 2 + hh
                total += jnp.dot(r_all[s, rows, :], m_of(pair, s), preferred_element_type=F32)
            prod[pair, rows, :] = total
            p_send[2 * pair, rows, :] = total[:, :128].astype(BF)
            p_send[2 * pair + 1, rows, :] = total[:, 128:].astype(BF)
            return carry

        lax.fori_loop(0, 4, body, 0)

    def part(chunk, rows):
        return prod[chunk // 2, rows, pl.ds((chunk % 2) * 128, 128)]

    def half_rows(quarter, half):
        return at(quarter * 256 + half * 128, 128)

    def y_out(chunk, slot, value, to):
        y_send[chunk, slot - 4] = value.astype(BF)
        ycopy[chunk, slot] = send(y_send.at[chunk, slot - 4], y_recv.at[chunk, slot], to)

    def p_out(chunk, slot, quarter, half, to):
        ycopy[chunk, slot] = send(
            p_send.at[chunk, half_rows(quarter, half)], y_recv.at[chunk, slot], to
        )

    def stage_a(chunk):
        if chunk % 2 == 0:
            finish(chunk // 2)
        p_out(chunk, 0, y_far, 0, to_yu)
        p_out(chunk, 1, y_far, 1, to_yd)
        p_out(chunk, 2, y_up, 1, to_yu)
        p_out(chunk, 3, y_dn, 0, to_yd)

    def stage_b(chunk):
        ycopy[chunk, 0].wait_recv()
        value = part(chunk, half_rows(y_up, 0)) + y_recv[chunk, 0].astype(F32)
        y_out(chunk, 4, value, to_yu)
        ycopy[chunk, 1].wait_recv()
        value = part(chunk, half_rows(y_dn, 1)) + y_recv[chunk, 1].astype(F32)
        y_out(chunk, 5, value, to_yd)

    def o_copy(chunk, slot, quarter, half, to):
        ref = o_all.at[chunk, half_rows(quarter, half)]
        ycopy[chunk, slot] = send(ref, ref, to)

    def stage_c(chunk):
        ycopy[chunk, 3].wait_recv()
        ycopy[chunk, 4].wait_recv()
        o_all[chunk, half_rows(y, 0), :] = (
            part(chunk, half_rows(y, 0)) + y_recv[chunk, 3].astype(F32) + y_recv[chunk, 4].astype(F32)
        ).astype(BF)
        o_copy(chunk, 6, y, 0, to_yu)
        ycopy[chunk, 2].wait_recv()
        ycopy[chunk, 5].wait_recv()
        o_all[chunk, half_rows(y, 1), :] = (
            part(chunk, half_rows(y, 1)) + y_recv[chunk, 2].astype(F32) + y_recv[chunk, 5].astype(F32)
        ).astype(BF)
        o_copy(chunk, 7, y, 1, to_yd)
        o_copy(chunk, 8, y, 1, to_yu)
        o_copy(chunk, 9, y, 0, to_yd)

    def stage_d(chunk):
        ycopy[chunk, 6].wait_recv()
        o_copy(chunk, 10, y_dn, 0, to_yu)
        ycopy[chunk, 7].wait_recv()
        o_copy(chunk, 11, y_up, 1, to_yd)

    def z_out(chunk, slot, size, value, to):
        if slot % 4 == 3:
            src, dst = z_last_send.at[chunk, slot // 4], z_last_recv.at[chunk, slot // 4]
            src[...] = value
        else:
            part = pl.ds(0, size)
            src, dst = z_send.at[chunk, slot, part], z_recv.at[chunk, slot, part]
            src[...] = value.astype(BF)
        zcopy[chunk, slot] = send(src, dst, to)

    def stage_e(chunk):
        for slot in (8, 9, 10, 11):
            ycopy[chunk, slot].wait_recv()

        def multiply(i):
            rows = at(i * 512, 512)
            d_all[chunk, rows, :] = jnp.dot(mr_all[rows, :], o_all[chunk], preferred_element_type=F32)

        far = (z + 4) % NZ
        multiply(far // 4)
        z_out(chunk, 0, 64, d_all[chunk, at(far * 128, 64), :], to_zu)
        z_out(chunk, 4, 64, d_all[chunk, at(far * 128 + 64, 64), :], to_zd)
        multiply(1 - far // 4)

    def stage_f(chunk, step):
        for slot, ahead, to in ((step, 4 - step, to_zu), (4 + step, 4 + step, to_zd)):
            zcopy[chunk, slot - 1].wait_recv()
            base = ((z + ahead) % NZ) * 128
            if step == 1:
                halves = [d_all[chunk, at(base, 64), :], d_all[chunk, at(base + 64, 64), :]]
                halves[slot // 4] += z_recv[chunk, slot - 1, pl.ds(0, 64), :].astype(F32)
                value = jnp.concatenate(halves, axis=0)
            else:
                value = d_all[chunk, at(base, 128), :] + z_recv[chunk, slot - 1].astype(F32)
            z_out(chunk, slot, 128, value, to)

    e_copies, w_copies = {}, []

    def d_there(chunk):
        return pltpu.make_async_remote_copy(
            src_ref=d_send.at[chunk],
            dst_ref=d_here.at[at(e_slot * 128, 128)],
            send_sem=d_send_sems.at[chunk],
            recv_sem=d_recv_sems.at[e_slot],
            device_id=device(x, chunk, h, z),
            device_id_type=MESH,
        )

    def stage_g(chunk):
        zcopy[chunk, 3].wait_recv()
        zcopy[chunk, 7].wait_recv()
        value = d_all[chunk, at(z * 128, 128), :] + z_last_recv[chunk, 0] + z_last_recv[chunk, 1]
        value += child_all[chunk]
        ref = w_all.at[h, chunk, x]
        ref[...] = value.astype(BF)
        for k in (2, 1, 3):
            e_copies[chunk, k] = send(ref, ref, device((x + k) % NX, y, h, z))
        d_send[chunk] = value

        @pl.when(y == chunk)
        def _():
            here = d_here.at[at(e_slot * 128, 128)]
            pltpu.make_async_copy(d_send.at[chunk], here, d_recv_sems.at[e_slot]).start()

        @pl.when(y != chunk)
        def _():
            d_there(chunk).start()

    def stage_h(chunk):
        for k in (1, 3, 2):
            e_copies[chunk, k].wait_recv()
        w_copies.append(send(w_all.at[h, chunk], w_all.at[h, chunk], sib))

    stages = [stage_a, stage_b, stage_c, stage_d, stage_e]
    stages += [functools.partial(stage_f, step=step) for step in (1, 2, 3)]
    stages += [stage_g, stage_h]
    for step in range(len(stages) + NY - 1):
        order = [chunk for chunk in range(NY) if 0 <= step - chunk < len(stages)]
        if step >= NY:
            order = order[::-1]
        if step == 2:
            t0.wait_recv()
            t2 = send(mr_half(seg_dn, 0), mr_half(seg_dn, 0), to_xu)
            t5 = send(mr_rows(seg_dn), mr_rows(seg_dn), sib)
            t1.wait_recv()
            t3 = send(mr_half(seg_up, 1), mr_half(seg_up, 1), to_xd)
            t6 = send(mr_rows(seg_up), mr_rows(seg_up), sib)
        if step == 8:
            for copy in child_copies:
                copy.wait_recv()
        if step == 4:
            t2.wait_recv()
            t3.wait_recv()
            t7 = send(mr_rows(seg_far), mr_rows(seg_far), sib)
        for chunk in order:
            if step == 4 and chunk == 0:
                for copy in (t4, t5, t6, t7):
                    copy.wait_recv()
            stages[step - chunk](chunk)

    for copy in w_copies:
        copy.wait_recv()
    own_rows = own_all.at[at(e_slot * 128, 128)]

    def owned_by(yy):
        t = owner[(x * NY + yy) * 2 + h]
        return w_all[t % 2, (t // 2) % NY, t // (2 * NY)]

    last_copies = []
    for k in (2, 1, 3):
        yy = (y + k) % NY
        last_send[k - 1] = owned_by(yy)
        last_copies.append(send(last_send.at[k - 1], own_rows, device(x, yy, h, z)))
    own_rows[...] = owned_by(y)
    off_out[...] = o_all[y]
    for slot in range(4):
        ref = d_here.at[pl.ds(slot * 128, 128)]
        pltpu.make_async_copy(ref, ref, d_recv_sems.at[slot]).wait()
    diag_out[...] = d_here[...]
    for copy in last_copies:
        copy.wait_recv()
    own_out[...] = own_all[...]

    links.drain()
    for chunk in range(NY):

        @pl.when(y != chunk)
        def _(chunk=chunk):
            d_there(chunk).wait_send()

    @pl.when(jnp.logical_not(stays))
    def _():
        swap().wait_send()


def outputs(off, diag, own, off_out, diag_out, own_out):
    off_out[...] = -off[...].astype(F32)
    diag_out[...] = diag[...]
    for i in range(4):
        rows = pl.ds(i * 128, 128)
        own_out[:, rows] = own[rows, :].astype(F32).T.astype(BF)


def on_device(root_inv, panel, pattern, child_diag, owner):
    vmem = pl.BlockSpec(memory_space=pltpu.VMEM)
    smem = pl.BlockSpec(memory_space=pltpu.SMEM)
    hbm = pl.BlockSpec(memory_space=pl.ANY)
    off, diag, own = pl.pallas_call(
        kernel,
        out_shape=(
            jax.ShapeDtypeStruct((1024, 128), BF),
            jax.ShapeDtypeStruct((512, 128), F32),
            jax.ShapeDtypeStruct((512, 128), BF),
        ),
        in_specs=[hbm, hbm, smem, hbm, smem],
        out_specs=(vmem, vmem, vmem),
        scratch_shapes=[
            pltpu.VMEM((8, 1024, 256), BF),
            pltpu.VMEM((8192, 128), BF),
            pltpu.VMEM((len(DIRECT), NY - 1, 256, 128), BF),
            pltpu.VMEM((2, 2048, 256), BF),
            pltpu.VMEM((128, 1024), BF),
            pltpu.VMEM((1024, 1024), BF),
            pltpu.VMEM((512, 128), F32),
            pltpu.VMEM((NY, 128, 128), F32),
            pltpu.VMEM((2, 1024, 256), F32),
            pltpu.VMEM((NY, 1024, 128), BF),
            pltpu.VMEM((NY, 2, 128, 128), BF),
            pltpu.VMEM((NY, 6, 128, 128), BF),
            pltpu.VMEM((NY, 1024, 128), BF),
            pltpu.VMEM((NY, 1024, 128), F32),
            pltpu.VMEM((NY, 7, 128, 128), BF),
            pltpu.VMEM((NY, 7, 128, 128), BF),
            pltpu.VMEM((NY, 2, 128, 128), F32),
            pltpu.VMEM((NY, 2, 128, 128), F32),
            pltpu.VMEM((NY, 128, 128), F32),
            pltpu.VMEM((512, 128), F32),
            pltpu.VMEM((2, NY, NX, 128, 128), BF),
            pltpu.VMEM((NY - 1, 128, 128), BF),
            pltpu.VMEM((512, 128), BF),
            pltpu.SemaphoreType.DMA((N_LINKS,)),
            pltpu.SemaphoreType.DMA((N_LINKS,)),
            pltpu.SemaphoreType.DMA((2,)),
            pltpu.SemaphoreType.DMA((NY,)),
            pltpu.SemaphoreType.DMA((4,)),
            pltpu.SemaphoreType.DMA((3,)),
        ],
        compiler_params=pltpu.CompilerParams(
            collective_id=0, has_side_effects=True, vmem_limit_bytes=60 * 1024 * 1024
        ),
    )(root_inv, panel, pattern.T, child_diag, owner)
    return pl.pallas_call(
        outputs,
        out_shape=(
            jax.ShapeDtypeStruct((1024, 128), F32),
            jax.ShapeDtypeStruct((512, 128), F32),
            jax.ShapeDtypeStruct((128, 512), BF),
        ),
        in_specs=[vmem] * 3,
        out_specs=(vmem,) * 3,
        compiler_params=pltpu.CompilerParams(vmem_limit_bytes=60 * 1024 * 1024),
    )(off, diag, own)


def solution(mesh):
    placed = (P("row", "col"), P(None, "col"), P(), P("row", "col"), P())
    return jax.shard_map(
        on_device,
        mesh=mesh,
        in_specs=placed,
        out_specs=(P("row", "col"), P("row", "col"), P("col", "row")),
        check_vma=False,
    )
```

```python
import functools

import jax
import jax.numpy as jnp
from jax import lax
from jax.experimental import pallas as pl
from jax.experimental.pallas import tpu as pltpu
from jax.sharding import PartitionSpec as P

MESH = pl.DeviceIdType.MESH
BF = jnp.bfloat16
F32 = jnp.float32

NX, NY, NZ = 4, 4, 8
Z_STEPS = 2
DIRECT = (0, 3, 4, 5)


def at(start, size):
    return pl.ds(pl.multiple_of(start, size), size)


class Links:
    def __init__(self, send_sems, recv_sems):
        self.send_sems, self.recv_sems = send_sems, recv_sems
        self.count = 0
        self.started = []

    def send(self, src, dst, device):
        index = self.count
        self.count += 1
        copy = pltpu.make_async_remote_copy(
            src_ref=src,
            dst_ref=dst,
            send_sem=self.send_sems.at[index],
            recv_sem=self.recv_sems.at[index],
            device_id=device,
            device_id_type=MESH,
        )
        copy.start()
        self.started.append(copy)
        return copy

    def drain(self):
        for copy in self.started:
            copy.wait_send()


N_LINKS = 11 + 8 + 3 + 3 * len(DIRECT) + 4 * Z_STEPS + NY * (12 + 8 + 3 + 1) + 3


def kernel(
    root, panel, pattern, child, owner,
    off_out, diag_out, own_out,
    r_all, panel_v, m_send, m_all, mr_own, mr_all, child_v, child_all,
    prod, p_send, y_send, y_recv, o_all, d_all, z_send, z_recv, z_last_send, z_last_recv,
    d_send, d_here, w_all, last_send, own_all,
    send_sems, recv_sems, swap_sems, d_send_sems, d_recv_sems, local_sems,
):
    z = lax.axis_index("row")
    c = lax.axis_index("col")
    h = c % 2
    y = (c // 2) % NY
    x = c // (2 * NY)

    def device(xx, yy, hh, zz):
        return (zz, (xx * NY + yy) * 2 + hh)

    def wrap(value, size):
        return (value + size) % size

    x_up, x_dn, x_far = wrap(x + 1, NX), wrap(x - 1, NX), wrap(x + 2, NX)
    y_up, y_dn, y_far = wrap(y + 1, NY), wrap(y - 1, NY), wrap(y + 2, NY)
    z_up, z_dn = wrap(z + 1, NZ), wrap(z - 1, NZ)
    sib = device(x, y, 1 - h, z)
    to_xu, to_xd = device(x_up, y, h, z), device(x_dn, y, h, z)
    to_yu, to_yd = device(x, y_up, h, z), device(x, y_dn, h, z)
    to_zu, to_zd = device(x, y, h, z_up), device(x, y, h, z_dn)

    links = Links(send_sems, recv_sems)
    send = links.send

    seg_own = x * 2 + h
    own_r = pltpu.make_async_copy(root, r_all.at[seg_own], local_sems.at[0])
    own_r.start()
    own_panel = pltpu.make_async_copy(panel, panel_v, local_sems.at[1])
    own_panel.start()
    own_child = pltpu.make_async_copy(child, child_v, local_sems.at[2])
    own_child.start()

    barrier = pltpu.get_barrier_semaphore()
    partner = device(x, y_far, 1 - h, z)
    peers = [sib, partner, to_xu, to_xd, device(x_far, y, h, z), to_zu, to_zd]
    peers += [device(x, (y + k) % NY, h, z) for k in range(1, NY)]
    for peer in peers:
        pl.semaphore_signal(barrier, inc=1, device_id=peer, device_id_type=MESH)
    pl.semaphore_wait(barrier, len(peers))

    top, low = pl.ds(0, 512), pl.ds(512, 512)
    r0 = send(root.at[top], r_all.at[seg_own, top], to_xu)
    r1 = send(root.at[low], r_all.at[seg_own, low], to_xd)
    r6 = send(root, r_all.at[seg_own], sib)

    own_panel.wait()

    def mask_into(dst_of, first_row, blocks):
        def body(i, carry):
            row = first_row + i * 128
            on = pattern[c, row // 128].astype(F32)
            value = panel_v[at(row, 128), :].astype(F32) * on
            dst_of(i, value)
            return carry

        lax.fori_loop(0, blocks, body, 0)

    def segment_row(s, yy):
        return (((s // 2) * NY + yy) * 2 + s % 2) * 256

    own_lanes, other_lanes = at((y % 2) * 128, 128), at(((y + 1) % 2) * 128, 128)
    m_copies = {}

    def over_y(i):
        s = (z + DIRECT[i]) % NZ
        for k in range(1, NY):

            def put(b, value):
                m_send[i, k - 1, at(b * 128, 128), :] = value.astype(BF)

            mask_into(put, segment_row(s, (y + k) % NY), 2)
            m_copies[i, k] = send(
                m_send.at[i, k - 1],
                m_all.at[y // 2, at(s * 256, 256), own_lanes],
                device(x, (y + k) % NY, h, z),
            )

    over_y(0)
    def own_segment(s, carry):
        def put(b, value):
            m_all[y // 2, at(s * 256 + b * 128, 128), own_lanes] = value.astype(BF)

        mask_into(put, segment_row(s, y), 2)
        return carry

    lax.fori_loop(0, 8, own_segment, 0)

    r2 = send(root.at[low], r_all.at[seg_own, low], to_xu)
    r3 = send(root.at[top], r_all.at[seg_own, top], to_xd)

    def put_transposed(b, value):
        mr_own[:, at(b * 128, 128)] = value.T.astype(BF)

    mask_into(put_transposed, z * 1024, 8)
    stays = h == y // 2

    def swap():
        return pltpu.make_async_remote_copy(
            src_ref=mr_own,
            dst_ref=mr_all.at[at((x * 2 + 1 - h) * 128, 128)],
            send_sem=swap_sems.at[0],
            recv_sem=swap_sems.at[1],
            device_id=partner,
            device_id_type=MESH,
        )

    def slot_of(yy):
        return 2 * (yy % 2) + yy // 2

    def along_z(s, i, to):
        rows = at(s * 256, 256)
        ref = m_all.at[y // 2, rows, other_lanes] if i == 0 else m_all.at[1 - y // 2, rows]
        return send(ref, ref, to)

    def arrived(copies):
        for copy in copies:
            copy.wait_recv()

    for k in range(1, NY):
        m_copies[0, k].wait_recv()
    up, down = [], []
    for i in range(2):
        up.append(along_z(z, i, to_zu))
        down.append(along_z(z, i, to_zd))
    for i in range(1, len(DIRECT)):
        over_y(i)
    own_child.wait()
    e_slot = slot_of(y)
    child_all[y] = child_v[at(e_slot * 128, 128), :]

    r0.wait_recv()
    seg_dn, seg_up, seg_far = x_dn * 2 + h, x_up * 2 + h, x_far * 2 + h
    r4 = send(r_all.at[seg_dn, top], r_all.at[seg_dn, top], to_xu)
    r1.wait_recv()
    r5 = send(r_all.at[seg_up, low], r_all.at[seg_up, low], to_xd)

    for step in range(1, Z_STEPS):
        for i in range(2):
            up[i].wait_recv()
            up[i] = along_z(wrap(z - step, NZ), i, to_zu)
            down[i].wait_recv()
            down[i] = along_z(wrap(z + step, NZ), i, to_zd)

    r2.wait_recv()
    r7 = send(r_all.at[seg_dn], r_all.at[seg_dn], sib)
    r3.wait_recv()
    r8 = send(r_all.at[seg_up], r_all.at[seg_up], sib)

    def mr_rows(s):
        return mr_all.at[at(s * 128, 128)]

    def mr_half(s, half):
        return mr_all.at[at(s * 128 + half * 64, 64)]

    @pl.when(stays)
    def _():
        pltpu.make_async_copy(mr_own, mr_all.at[at(seg_own * 128, 128)], swap_sems.at[1]).start()

    @pl.when(jnp.logical_not(stays))
    def _():
        swap().start()

    arrived(up)
    arrived(down)
    for i in range(1, len(DIRECT)):
        for k in range(1, NY):
            m_copies[i, k].wait_recv()
    child_copies = []
    for k in range(1, NY):
        yy = (y + k) % NY
        child_copies.append(
            send(child_v.at[at(slot_of(yy) * 128, 128)], child_all.at[y], device(x, yy, h, z))
        )
    own_r.wait()
    r6.wait_recv()
    r7.wait_recv()
    r8.wait_recv()

    def m_of(pair, s):
        return m_all[pair, at(s * 256, 256), :]

    def first_product(i, carry):
        pair, rows = i // 4, at((i % 4) * 256, 256)
        total = None
        for xx in (x, x_dn, x_up):
            for hh in range(2):
                s = xx * 2 + hh
                term = jnp.dot(r_all[s, rows, :], m_of(pair, s), preferred_element_type=F32)
                total = term if total is None else total + term
        prod[pair, rows, :] = total
        return carry

    lax.fori_loop(0, 4, first_product, 0)

    r4.wait_recv()
    r9 = send(r_all.at[seg_far, top], r_all.at[seg_far, top], sib)
    r5.wait_recv()
    r10 = send(r_all.at[seg_far, low], r_all.at[seg_far, low], sib)

    lax.fori_loop(4, 8, first_product, 0)
    pltpu.make_async_copy(mr_own, mr_rows(seg_own), swap_sems.at[1]).wait()
    t0 = send(mr_rows(seg_own), mr_rows(seg_own), to_xu)
    t1 = send(mr_rows(seg_own), mr_rows(seg_own), to_xd)
    t4 = send(mr_rows(seg_own), mr_rows(seg_own), sib)

    r9.wait_recv()
    r10.wait_recv()

    ycopy, zcopy = {}, {}

    def finish(pair):
        def body(quarter, carry):
            rows = at(quarter * 256, 256)
            total = prod[pair, rows, :]
            for hh in range(2):
                s = x_far * 2 + hh
                total += jnp.dot(r_all[s, rows, :], m_of(pair, s), preferred_element_type=F32)
            prod[pair, rows, :] = total
            p_send[2 * pair, rows, :] = total[:, :128].astype(BF)
            p_send[2 * pair + 1, rows, :] = total[:, 128:].astype(BF)
            return carry

        lax.fori_loop(0, 4, body, 0)

    def part(chunk, rows):
        return prod[chunk // 2, rows, pl.ds((chunk % 2) * 128, 128)]

    def half_rows(quarter, half):
        return at(quarter * 256 + half * 128, 128)

    def y_out(chunk, slot, value, to):
        y_send[chunk, slot - 4] = value.astype(BF)
        ycopy[chunk, slot] = send(y_send.at[chunk, slot - 4], y_recv.at[chunk, slot], to)

    def p_out(chunk, slot, quarter, half, to):
        ycopy[chunk, slot] = send(
            p_send.at[chunk, half_rows(quarter, half)], y_recv.at[chunk, slot], to
        )

    def stage_a(chunk):
        if chunk % 2 == 0:
            finish(chunk // 2)
        p_out(chunk, 0, y_far, 0, to_yu)
        p_out(chunk, 1, y_far, 1, to_yd)
        p_out(chunk, 2, y_up, 1, to_yu)
        p_out(chunk, 3, y_dn, 0, to_yd)

    def stage_b(chunk):
        ycopy[chunk, 0].wait_recv()
        value = part(chunk, half_rows(y_up, 0)) + y_recv[chunk, 0].astype(F32)
        y_out(chunk, 4, value, to_yu)
        ycopy[chunk, 1].wait_recv()
        value = part(chunk, half_rows(y_dn, 1)) + y_recv[chunk, 1].astype(F32)
        y_out(chunk, 5, value, to_yd)

    def o_copy(chunk, slot, quarter, half, to):
        ref = o_all.at[chunk, half_rows(quarter, half)]
        ycopy[chunk, slot] = send(ref, ref, to)

    def stage_c(chunk):
        ycopy[chunk, 3].wait_recv()
        ycopy[chunk, 4].wait_recv()
        o_all[chunk, half_rows(y, 0), :] = (
            part(chunk, half_rows(y, 0)) + y_recv[chunk, 3].astype(F32) + y_recv[chunk, 4].astype(F32)
        ).astype(BF)
        o_copy(chunk, 6, y, 0, to_yu)
        ycopy[chunk, 2].wait_recv()
        ycopy[chunk, 5].wait_recv()
        o_all[chunk, half_rows(y, 1), :] = (
            part(chunk, half_rows(y, 1)) + y_recv[chunk, 2].astype(F32) + y_recv[chunk, 5].astype(F32)
        ).astype(BF)
        o_copy(chunk, 7, y, 1, to_yd)
        o_copy(chunk, 8, y, 1, to_yu)
        o_copy(chunk, 9, y, 0, to_yd)

    def stage_d(chunk):
        ycopy[chunk, 6].wait_recv()
        o_copy(chunk, 10, y_dn, 0, to_yu)
        ycopy[chunk, 7].wait_recv()
        o_copy(chunk, 11, y_up, 1, to_yd)

    def z_out(chunk, slot, size, value, to):
        if slot % 4 == 3:
            src, dst = z_last_send.at[chunk, slot // 4], z_last_recv.at[chunk, slot // 4]
            src[...] = value
        else:
            part = pl.ds(0, size)
            src, dst = z_send.at[chunk, slot, part], z_recv.at[chunk, slot, part]
            src[...] = value.astype(BF)
        zcopy[chunk, slot] = send(src, dst, to)

    def stage_e(chunk):
        for slot in (8, 9, 10, 11):
            ycopy[chunk, slot].wait_recv()

        def multiply(i):
            rows = at(i * 512, 512)
            d_all[chunk, rows, :] = jnp.dot(mr_all[rows, :], o_all[chunk], preferred_element_type=F32)

        far = (z + 4) % NZ
        multiply(far // 4)
        z_out(chunk, 0, 64, d_all[chunk, at(far * 128, 64), :], to_zu)
        z_out(chunk, 4, 64, d_all[chunk, at(far * 128 + 64, 64), :], to_zd)
        multiply(1 - far // 4)

    def stage_f(chunk, step):
        for slot, ahead, to in ((step, 4 - step, to_zu), (4 + step, 4 + step, to_zd)):
            zcopy[chunk, slot - 1].wait_recv()
            base = ((z + ahead) % NZ) * 128
            if step == 1:
                halves = [d_all[chunk, at(base, 64), :], d_all[chunk, at(base + 64, 64), :]]
                halves[slot // 4] += z_recv[chunk, slot - 1, pl.ds(0, 64), :].astype(F32)
                value = jnp.concatenate(halves, axis=0)
            else:
                value = d_all[chunk, at(base, 128), :] + z_recv[chunk, slot - 1].astype(F32)
            z_out(chunk, slot, 128, value, to)

    e_copies, w_copies = {}, []

    def d_there(chunk):
        return pltpu.make_async_remote_copy(
            src_ref=d_send.at[chunk],
            dst_ref=d_here.at[at(e_slot * 128, 128)],
            send_sem=d_send_sems.at[chunk],
            recv_sem=d_recv_sems.at[e_slot],
            device_id=device(x, chunk, h, z),
            device_id_type=MESH,
        )

    def stage_g(chunk):
        zcopy[chunk, 3].wait_recv()
        zcopy[chunk, 7].wait_recv()
        value = d_all[chunk, at(z * 128, 128), :] + z_last_recv[chunk, 0] + z_last_recv[chunk, 1]
        value += child_all[chunk]
        ref = w_all.at[h, chunk, x]
        ref[...] = value.astype(BF)
        for k in (2, 1, 3):
            e_copies[chunk, k] = send(ref, ref, device((x + k) % NX, y, h, z))
        d_send[chunk] = value

        @pl.when(y == chunk)
        def _():
            here = d_here.at[at(e_slot * 128, 128)]
            pltpu.make_async_copy(d_send.at[chunk], here, d_recv_sems.at[e_slot]).start()

        @pl.when(y != chunk)
        def _():
            d_there(chunk).start()

    def stage_h(chunk):
        for k in (1, 3, 2):
            e_copies[chunk, k].wait_recv()
        w_copies.append(send(w_all.at[h, chunk], w_all.at[h, chunk], sib))

    stages = [stage_a, stage_b, stage_c, stage_d, stage_e]
    stages += [functools.partial(stage_f, step=step) for step in (1, 2, 3)]
    stages += [stage_g, stage_h]
    for step in range(len(stages) + NY - 1):
        order = [chunk for chunk in range(NY) if 0 <= step - chunk < len(stages)]
        if step >= 3:
            order = order[::-1]
        if step == 2:
            t0.wait_recv()
            t2 = send(mr_half(seg_dn, 0), mr_half(seg_dn, 0), to_xu)
            t5 = send(mr_rows(seg_dn), mr_rows(seg_dn), sib)
            t1.wait_recv()
            t3 = send(mr_half(seg_up, 1), mr_half(seg_up, 1), to_xd)
            t6 = send(mr_rows(seg_up), mr_rows(seg_up), sib)
        if step == 8:
            for copy in child_copies:
                copy.wait_recv()
        if step == 4:
            t2.wait_recv()
            t3.wait_recv()
            t7 = send(mr_rows(seg_far), mr_rows(seg_far), sib)
        for chunk in order:
            if step == 4 and chunk == 0:
                for copy in (t4, t5, t6, t7):
                    copy.wait_recv()
            stages[step - chunk](chunk)

    for copy in w_copies:
        copy.wait_recv()
    own_rows = own_all.at[at(e_slot * 128, 128)]

    def owned_by(yy):
        t = owner[(x * NY + yy) * 2 + h]
        return w_all[t % 2, (t // 2) % NY, t // (2 * NY)]

    last_copies = []
    for k in (2, 1, 3):
        yy = (y + k) % NY
        last_send[k - 1] = owned_by(yy)
        last_copies.append(send(last_send.at[k - 1], own_rows, device(x, yy, h, z)))
    own_rows[...] = owned_by(y)
    off_out[...] = o_all[y]
    for slot in range(4):
        ref = d_here.at[pl.ds(slot * 128, 128)]
        pltpu.make_async_copy(ref, ref, d_recv_sems.at[slot]).wait()
    diag_out[...] = d_here[...]
    for copy in last_copies:
        copy.wait_recv()
    own_out[...] = own_all[...]

    links.drain()
    for chunk in range(NY):

        @pl.when(y != chunk)
        def _(chunk=chunk):
            d_there(chunk).wait_send()

    @pl.when(jnp.logical_not(stays))
    def _():
        swap().wait_send()


def outputs(off, diag, own, off_out, diag_out, own_out):
    off_out[...] = -off[...].astype(F32)
    diag_out[...] = diag[...]
    for i in range(4):
        rows = pl.ds(i * 128, 128)
        own_out[:, rows] = own[rows, :].astype(F32).T.astype(BF)


def on_device(root_inv, panel, pattern, child_diag, owner):
    vmem = pl.BlockSpec(memory_space=pltpu.VMEM)
    smem = pl.BlockSpec(memory_space=pltpu.SMEM)
    hbm = pl.BlockSpec(memory_space=pl.ANY)
    off, diag, own = pl.pallas_call(
        kernel,
        out_shape=(
            jax.ShapeDtypeStruct((1024, 128), BF),
            jax.ShapeDtypeStruct((512, 128), F32),
            jax.ShapeDtypeStruct((512, 128), BF),
        ),
        in_specs=[hbm, hbm, smem, hbm, smem],
        out_specs=(vmem, vmem, vmem),
        scratch_shapes=[
            pltpu.VMEM((8, 1024, 256), BF),
            pltpu.VMEM((8192, 128), BF),
            pltpu.VMEM((len(DIRECT), NY - 1, 256, 128), BF),
            pltpu.VMEM((2, 2048, 256), BF),
            pltpu.VMEM((128, 1024), BF),
            pltpu.VMEM((1024, 1024), BF),
            pltpu.VMEM((512, 128), F32),
            pltpu.VMEM((NY, 128, 128), F32),
            pltpu.VMEM((2, 1024, 256), F32),
            pltpu.VMEM((NY, 1024, 128), BF),
            pltpu.VMEM((NY, 2, 128, 128), BF),
            pltpu.VMEM((NY, 6, 128, 128), BF),
            pltpu.VMEM((NY, 1024, 128), BF),
            pltpu.VMEM((NY, 1024, 128), F32),
            pltpu.VMEM((NY, 7, 128, 128), BF),
            pltpu.VMEM((NY, 7, 128, 128), BF),
            pltpu.VMEM((NY, 2, 128, 128), F32),
            pltpu.VMEM((NY, 2, 128, 128), F32),
            pltpu.VMEM((NY, 128, 128), F32),
            pltpu.VMEM((512, 128), F32),
            pltpu.VMEM((2, NY, NX, 128, 128), BF),
            pltpu.VMEM((NY - 1, 128, 128), BF),
            pltpu.VMEM((512, 128), BF),
            pltpu.SemaphoreType.DMA((N_LINKS,)),
            pltpu.SemaphoreType.DMA((N_LINKS,)),
            pltpu.SemaphoreType.DMA((2,)),
            pltpu.SemaphoreType.DMA((NY,)),
            pltpu.SemaphoreType.DMA((4,)),
            pltpu.SemaphoreType.DMA((3,)),
        ],
        compiler_params=pltpu.CompilerParams(
            collective_id=0, has_side_effects=True, vmem_limit_bytes=60 * 1024 * 1024
        ),
    )(root_inv, panel, pattern.T, child_diag, owner)
    return pl.pallas_call(
        outputs,
        out_shape=(
            jax.ShapeDtypeStruct((1024, 128), F32),
            jax.ShapeDtypeStruct((512, 128), F32),
            jax.ShapeDtypeStruct((128, 512), BF),
        ),
        in_specs=[vmem] * 3,
        out_specs=(vmem,) * 3,
        compiler_params=pltpu.CompilerParams(vmem_limit_bytes=60 * 1024 * 1024),
    )(off, diag, own)


def solution(mesh):
    placed = (P("row", "col"), P(None, "col"), P(), P("row", "col"), P())
    return jax.shard_map(
        on_device,
        mesh=mesh,
        in_specs=placed,
        out_specs=(P("row", "col"), P("row", "col"), P("col", "row")),
        check_vma=False,
    )
```

```python
import functools

import jax
import jax.numpy as jnp
from jax import lax
from jax.experimental import pallas as pl
from jax.experimental.pallas import tpu as pltpu
from jax.sharding import PartitionSpec as P

MESH = pl.DeviceIdType.MESH
BF = jnp.bfloat16
F32 = jnp.float32

NX, NY, NZ = 4, 4, 8
Z_STEPS = 2
DIRECT = (0, 3, 4, 5)


def at(start, size):
    return pl.ds(pl.multiple_of(start, size), size)


class Links:
    def __init__(self, send_sems, recv_sems):
        self.send_sems, self.recv_sems = send_sems, recv_sems
        self.count = 0
        self.started = []

    def send(self, src, dst, device):
        index = self.count
        self.count += 1
        copy = pltpu.make_async_remote_copy(
            src_ref=src,
            dst_ref=dst,
            send_sem=self.send_sems.at[index],
            recv_sem=self.recv_sems.at[index],
            device_id=device,
            device_id_type=MESH,
        )
        copy.start()
        self.started.append(copy)
        return copy

    def drain(self):
        for copy in self.started:
            copy.wait_send()


N_LINKS = 11 + 8 + 3 + 3 * len(DIRECT) + 4 * Z_STEPS + NY * (12 + 8 + 3 + 1) + 3


def kernel(
    root, panel, pattern, child, owner,
    off_out, diag_out, own_out,
    r_all, panel_v, m_send, m_all, mr_own, mr_all, child_v, child_all,
    prod, p_send, y_send, y_recv, o_all, d_all, z_send, z_recv, z_last_send, z_last_recv,
    d_send, d_here, w_all, last_send, own_all,
    send_sems, recv_sems, swap_sems, d_send_sems, d_recv_sems, local_sems,
):
    z = lax.axis_index("row")
    c = lax.axis_index("col")
    h = c % 2
    y = (c // 2) % NY
    x = c // (2 * NY)

    def device(xx, yy, hh, zz):
        return (zz, (xx * NY + yy) * 2 + hh)

    def wrap(value, size):
        return (value + size) % size

    x_up, x_dn, x_far = wrap(x + 1, NX), wrap(x - 1, NX), wrap(x + 2, NX)
    y_up, y_dn, y_far = wrap(y + 1, NY), wrap(y - 1, NY), wrap(y + 2, NY)
    z_up, z_dn = wrap(z + 1, NZ), wrap(z - 1, NZ)
    sib = device(x, y, 1 - h, z)
    to_xu, to_xd = device(x_up, y, h, z), device(x_dn, y, h, z)
    to_yu, to_yd = device(x, y_up, h, z), device(x, y_dn, h, z)
    to_zu, to_zd = device(x, y, h, z_up), device(x, y, h, z_dn)

    links = Links(send_sems, recv_sems)
    send = links.send

    seg_own = x * 2 + h
    own_r = pltpu.make_async_copy(root, r_all.at[seg_own], local_sems.at[0])
    own_r.start()
    own_panel = pltpu.make_async_copy(panel, panel_v, local_sems.at[1])
    own_panel.start()
    own_child = pltpu.make_async_copy(child, child_v, local_sems.at[2])
    own_child.start()

    barrier = pltpu.get_barrier_semaphore()
    partner = device(x, y_far, 1 - h, z)
    peers = [sib, partner, to_xu, to_xd, device(x_far, y, h, z), to_zu, to_zd]
    peers += [device(x, (y + k) % NY, h, z) for k in range(1, NY)]
    for peer in peers:
        pl.semaphore_signal(barrier, inc=1, device_id=peer, device_id_type=MESH)
    pl.semaphore_wait(barrier, len(peers))

    top, low = pl.ds(0, 512), pl.ds(512, 512)
    r0 = send(root.at[top], r_all.at[seg_own, top], to_xu)
    r1 = send(root.at[low], r_all.at[seg_own, low], to_xd)
    r6 = send(root, r_all.at[seg_own], sib)

    own_panel.wait()

    def mask_into(dst_of, first_row, blocks):
        def body(i, carry):
            row = first_row + i * 128
            on = pattern[c, row // 128].astype(F32)
            value = panel_v[at(row, 128), :].astype(F32) * on
            dst_of(i, value)
            return carry

        lax.fori_loop(0, blocks, body, 0)

    def segment_row(s, yy):
        return (((s // 2) * NY + yy) * 2 + s % 2) * 256

    own_lanes, other_lanes = at((y % 2) * 128, 128), at(((y + 1) % 2) * 128, 128)
    m_copies = {}

    def over_y(i):
        s = (z + DIRECT[i]) % NZ
        for k in range(1, NY):

            def put(b, value):
                m_send[i, k - 1, at(b * 128, 128), :] = value.astype(BF)

            mask_into(put, segment_row(s, (y + k) % NY), 2)
            m_copies[i, k] = send(
                m_send.at[i, k - 1],
                m_all.at[y // 2, at(s * 256, 256), own_lanes],
                device(x, (y + k) % NY, h, z),
            )

    over_y(0)
    def own_segment(s, carry):
        def put(b, value):
            m_all[y // 2, at(s * 256 + b * 128, 128), own_lanes] = value.astype(BF)

        mask_into(put, segment_row(s, y), 2)
        return carry

    lax.fori_loop(0, 8, own_segment, 0)

    r2 = send(root.at[low], r_all.at[seg_own, low], to_xu)
    r3 = send(root.at[top], r_all.at[seg_own, top], to_xd)

    def put_transposed(b, value):
        mr_own[:, at(b * 128, 128)] = value.T.astype(BF)

    mask_into(put_transposed, z * 1024, 8)
    stays = h == y // 2

    def swap():
        return pltpu.make_async_remote_copy(
            src_ref=mr_own,
            dst_ref=mr_all.at[at((x * 2 + 1 - h) * 128, 128)],
            send_sem=swap_sems.at[0],
            recv_sem=swap_sems.at[1],
            device_id=partner,
            device_id_type=MESH,
        )

    def slot_of(yy):
        return 2 * (yy % 2) + yy // 2

    def along_z(s, i, to):
        rows = at(s * 256, 256)
        ref = m_all.at[y // 2, rows, other_lanes] if i == 0 else m_all.at[1 - y // 2, rows]
        return send(ref, ref, to)

    def arrived(copies):
        for copy in copies:
            copy.wait_recv()

    for k in range(1, NY):
        m_copies[0, k].wait_recv()
    up, down = [], []
    for i in range(2):
        up.append(along_z(z, i, to_zu))
        down.append(along_z(z, i, to_zd))
    for i in range(1, len(DIRECT)):
        over_y(i)
    own_child.wait()
    e_slot = slot_of(y)
    child_all[y] = child_v[at(e_slot * 128, 128), :]

    r0.wait_recv()
    seg_dn, seg_up, seg_far = x_dn * 2 + h, x_up * 2 + h, x_far * 2 + h
    r4 = send(r_all.at[seg_dn, top], r_all.at[seg_dn, top], to_xu)
    r1.wait_recv()
    r5 = send(r_all.at[seg_up, low], r_all.at[seg_up, low], to_xd)

    for step in range(1, Z_STEPS):
        for i in range(2):
            up[i].wait_recv()
            up[i] = along_z(wrap(z - step, NZ), i, to_zu)
            down[i].wait_recv()
            down[i] = along_z(wrap(z + step, NZ), i, to_zd)

    r2.wait_recv()
    r7 = send(r_all.at[seg_dn], r_all.at[seg_dn], sib)
    r3.wait_recv()
    r8 = send(r_all.at[seg_up], r_all.at[seg_up], sib)

    def mr_rows(s):
        return mr_all.at[at(s * 128, 128)]

    def mr_half(s, half):
        return mr_all.at[at(s * 128 + half * 64, 64)]

    @pl.when(stays)
    def _():
        pltpu.make_async_copy(mr_own, mr_all.at[at(seg_own * 128, 128)], swap_sems.at[1]).start()

    @pl.when(jnp.logical_not(stays))
    def _():
        swap().start()

    r4.wait_recv()
    r9 = send(r_all.at[seg_far, top], r_all.at[seg_far, top], sib)
    r5.wait_recv()
    r10 = send(r_all.at[seg_far, low], r_all.at[seg_far, low], sib)

    arrived(up)
    arrived(down)
    for i in range(1, len(DIRECT)):
        for k in range(1, NY):
            m_copies[i, k].wait_recv()
    child_copies = []
    for k in range(1, NY):
        yy = (y + k) % NY
        child_copies.append(
            send(child_v.at[at(slot_of(yy) * 128, 128)], child_all.at[y], device(x, yy, h, z))
        )
    own_r.wait()
    r6.wait_recv()
    r7.wait_recv()
    r8.wait_recv()

    def m_of(pair, s):
        return m_all[pair, at(s * 256, 256), :]

    def first_product(i, carry):
        pair, rows = i // 4, at((i % 4) * 256, 256)
        total = None
        for xx in (x, x_dn, x_up):
            for hh in range(2):
                s = xx * 2 + hh
                term = jnp.dot(r_all[s, rows, :], m_of(pair, s), preferred_element_type=F32)
                total = term if total is None else total + term
        prod[pair, rows, :] = total
        return carry

    lax.fori_loop(0, 4, first_product, 0)

    lax.fori_loop(4, 8, first_product, 0)
    pltpu.make_async_copy(mr_own, mr_rows(seg_own), swap_sems.at[1]).wait()
    t0 = send(mr_rows(seg_own), mr_rows(seg_own), to_xu)
    t1 = send(mr_rows(seg_own), mr_rows(seg_own), to_xd)
    t4 = send(mr_rows(seg_own), mr_rows(seg_own), sib)

    r9.wait_recv()
    r10.wait_recv()

    ycopy, zcopy = {}, {}

    def finish(pair):
        def body(quarter, carry):
            rows = at(quarter * 256, 256)
            total = prod[pair, rows, :]
            for hh in range(2):
                s = x_far * 2 + hh
                total += jnp.dot(r_all[s, rows, :], m_of(pair, s), preferred_element_type=F32)
            prod[pair, rows, :] = total
            p_send[2 * pair, rows, :] = total[:, :128].astype(BF)
            p_send[2 * pair + 1, rows, :] = total[:, 128:].astype(BF)
            return carry

        lax.fori_loop(0, 4, body, 0)

    def part(chunk, rows):
        return prod[chunk // 2, rows, pl.ds((chunk % 2) * 128, 128)]

    def half_rows(quarter, half):
        return at(quarter * 256 + half * 128, 128)

    def y_out(chunk, slot, value, to):
        y_send[chunk, slot - 4] = value.astype(BF)
        ycopy[chunk, slot] = send(y_send.at[chunk, slot - 4], y_recv.at[chunk, slot], to)

    def p_out(chunk, slot, quarter, half, to):
        ycopy[chunk, slot] = send(
            p_send.at[chunk, half_rows(quarter, half)], y_recv.at[chunk, slot], to
        )

    def stage_a(chunk):
        if chunk % 2 == 0:
            finish(chunk // 2)
        p_out(chunk, 0, y_far, 0, to_yu)
        p_out(chunk, 1, y_far, 1, to_yd)
        p_out(chunk, 2, y_up, 1, to_yu)
        p_out(chunk, 3, y_dn, 0, to_yd)

    def stage_b(chunk):
        ycopy[chunk, 0].wait_recv()
        value = part(chunk, half_rows(y_up, 0)) + y_recv[chunk, 0].astype(F32)
        y_out(chunk, 4, value, to_yu)
        ycopy[chunk, 1].wait_recv()
        value = part(chunk, half_rows(y_dn, 1)) + y_recv[chunk, 1].astype(F32)
        y_out(chunk, 5, value, to_yd)

    def o_copy(chunk, slot, quarter, half, to):
        ref = o_all.at[chunk, half_rows(quarter, half)]
        ycopy[chunk, slot] = send(ref, ref, to)

    def stage_c(chunk):
        ycopy[chunk, 3].wait_recv()
        ycopy[chunk, 4].wait_recv()
        o_all[chunk, half_rows(y, 0), :] = (
            part(chunk, half_rows(y, 0)) + y_recv[chunk, 3].astype(F32) + y_recv[chunk, 4].astype(F32)
        ).astype(BF)
        o_copy(chunk, 6, y, 0, to_yu)
        ycopy[chunk, 2].wait_recv()
        ycopy[chunk, 5].wait_recv()
        o_all[chunk, half_rows(y, 1), :] = (
            part(chunk, half_rows(y, 1)) + y_recv[chunk, 2].astype(F32) + y_recv[chunk, 5].astype(F32)
        ).astype(BF)
        o_copy(chunk, 7, y, 1, to_yd)
        o_copy(chunk, 8, y, 1, to_yu)
        o_copy(chunk, 9, y, 0, to_yd)

    def stage_d(chunk):
        ycopy[chunk, 6].wait_recv()
        o_copy(chunk, 10, y_dn, 0, to_yu)
        ycopy[chunk, 7].wait_recv()
        o_copy(chunk, 11, y_up, 1, to_yd)

    def z_out(chunk, slot, size, value, to):
        if slot % 4 == 3:
            src, dst = z_last_send.at[chunk, slot // 4], z_last_recv.at[chunk, slot // 4]
            src[...] = value
        else:
            part = pl.ds(0, size)
            src, dst = z_send.at[chunk, slot, part], z_recv.at[chunk, slot, part]
            src[...] = value.astype(BF)
        zcopy[chunk, slot] = send(src, dst, to)

    def stage_e(chunk):
        for slot in (8, 9, 10, 11):
            ycopy[chunk, slot].wait_recv()

        def multiply(i):
            rows = at(i * 512, 512)
            d_all[chunk, rows, :] = jnp.dot(mr_all[rows, :], o_all[chunk], preferred_element_type=F32)

        far = (z + 4) % NZ
        multiply(far // 4)
        z_out(chunk, 0, 64, d_all[chunk, at(far * 128, 64), :], to_zu)
        z_out(chunk, 4, 64, d_all[chunk, at(far * 128 + 64, 64), :], to_zd)
        multiply(1 - far // 4)

    def stage_f(chunk, step):
        for slot, ahead, to in ((step, 4 - step, to_zu), (4 + step, 4 + step, to_zd)):
            zcopy[chunk, slot - 1].wait_recv()
            base = ((z + ahead) % NZ) * 128
            if step == 1:
                halves = [d_all[chunk, at(base, 64), :], d_all[chunk, at(base + 64, 64), :]]
                halves[slot // 4] += z_recv[chunk, slot - 1, pl.ds(0, 64), :].astype(F32)
                value = jnp.concatenate(halves, axis=0)
            else:
                value = d_all[chunk, at(base, 128), :] + z_recv[chunk, slot - 1].astype(F32)
            z_out(chunk, slot, 128, value, to)

    e_copies, w_copies = {}, []

    def d_there(chunk):
        return pltpu.make_async_remote_copy(
            src_ref=d_send.at[chunk],
            dst_ref=d_here.at[at(e_slot * 128, 128)],
            send_sem=d_send_sems.at[chunk],
            recv_sem=d_recv_sems.at[e_slot],
            device_id=device(x, chunk, h, z),
            device_id_type=MESH,
        )

    def stage_g(chunk):
        zcopy[chunk, 3].wait_recv()
        zcopy[chunk, 7].wait_recv()
        value = d_all[chunk, at(z * 128, 128), :] + z_last_recv[chunk, 0] + z_last_recv[chunk, 1]
        value += child_all[chunk]
        ref = w_all.at[h, chunk, x]
        ref[...] = value.astype(BF)
        for k in (2, 1, 3):
            e_copies[chunk, k] = send(ref, ref, device((x + k) % NX, y, h, z))
        d_send[chunk] = value

        @pl.when(y == chunk)
        def _():
            here = d_here.at[at(e_slot * 128, 128)]
            pltpu.make_async_copy(d_send.at[chunk], here, d_recv_sems.at[e_slot]).start()

        @pl.when(y != chunk)
        def _():
            d_there(chunk).start()

    def stage_h(chunk):
        for k in (1, 3, 2):
            e_copies[chunk, k].wait_recv()
        w_copies.append(send(w_all.at[h, chunk], w_all.at[h, chunk], sib))

    stages = [stage_a, stage_b, stage_c, stage_d, stage_e]
    stages += [functools.partial(stage_f, step=step) for step in (1, 2, 3)]
    stages += [stage_g, stage_h]
    for step in range(len(stages) + NY - 1):
        order = [chunk for chunk in range(NY) if 0 <= step - chunk < len(stages)]
        if step >= 3:
            order = order[::-1]
        if step == 2:
            t0.wait_recv()
            t2 = send(mr_half(seg_dn, 0), mr_half(seg_dn, 0), to_xu)
            t5 = send(mr_rows(seg_dn), mr_rows(seg_dn), sib)
            t1.wait_recv()
            t3 = send(mr_half(seg_up, 1), mr_half(seg_up, 1), to_xd)
            t6 = send(mr_rows(seg_up), mr_rows(seg_up), sib)
        if step == 8:
            for copy in child_copies:
                copy.wait_recv()
        if step == 4:
            t2.wait_recv()
            t3.wait_recv()
            t7 = send(mr_rows(seg_far), mr_rows(seg_far), sib)
        for chunk in order:
            if step == 4 and chunk == 0:
                for copy in (t4, t5, t6, t7):
                    copy.wait_recv()
            stages[step - chunk](chunk)

    for copy in w_copies:
        copy.wait_recv()
    own_rows = own_all.at[at(e_slot * 128, 128)]

    def owned_by(yy):
        t = owner[(x * NY + yy) * 2 + h]
        return w_all[t % 2, (t // 2) % NY, t // (2 * NY)]

    last_copies = []
    for k in (2, 1, 3):
        yy = (y + k) % NY
        last_send[k - 1] = owned_by(yy)
        last_copies.append(send(last_send.at[k - 1], own_rows, device(x, yy, h, z)))
    own_rows[...] = owned_by(y)
    off_out[...] = o_all[y]
    for slot in range(4):
        ref = d_here.at[pl.ds(slot * 128, 128)]
        pltpu.make_async_copy(ref, ref, d_recv_sems.at[slot]).wait()
    diag_out[...] = d_here[...]
    for copy in last_copies:
        copy.wait_recv()
    own_out[...] = own_all[...]

    links.drain()
    for chunk in range(NY):

        @pl.when(y != chunk)
        def _(chunk=chunk):
            d_there(chunk).wait_send()

    @pl.when(jnp.logical_not(stays))
    def _():
        swap().wait_send()


def outputs(off, diag, own, off_out, diag_out, own_out):
    off_out[...] = -off[...].astype(F32)
    diag_out[...] = diag[...]
    for i in range(4):
        rows = pl.ds(i * 128, 128)
        own_out[:, rows] = own[rows, :].astype(F32).T.astype(BF)


def on_device(root_inv, panel, pattern, child_diag, owner):
    vmem = pl.BlockSpec(memory_space=pltpu.VMEM)
    smem = pl.BlockSpec(memory_space=pltpu.SMEM)
    hbm = pl.BlockSpec(memory_space=pl.ANY)
    off, diag, own = pl.pallas_call(
        kernel,
        out_shape=(
            jax.ShapeDtypeStruct((1024, 128), BF),
            jax.ShapeDtypeStruct((512, 128), F32),
            jax.ShapeDtypeStruct((512, 128), BF),
        ),
        in_specs=[hbm, hbm, smem, hbm, smem],
        out_specs=(vmem, vmem, vmem),
        scratch_shapes=[
            pltpu.VMEM((8, 1024, 256), BF),
            pltpu.VMEM((8192, 128), BF),
            pltpu.VMEM((len(DIRECT), NY - 1, 256, 128), BF),
            pltpu.VMEM((2, 2048, 256), BF),
            pltpu.VMEM((128, 1024), BF),
            pltpu.VMEM((1024, 1024), BF),
            pltpu.VMEM((512, 128), F32),
            pltpu.VMEM((NY, 128, 128), F32),
            pltpu.VMEM((2, 1024, 256), F32),
            pltpu.VMEM((NY, 1024, 128), BF),
            pltpu.VMEM((NY, 2, 128, 128), BF),
            pltpu.VMEM((NY, 6, 128, 128), BF),
            pltpu.VMEM((NY, 1024, 128), BF),
            pltpu.VMEM((NY, 1024, 128), F32),
            pltpu.VMEM((NY, 7, 128, 128), BF),
            pltpu.VMEM((NY, 7, 128, 128), BF),
            pltpu.VMEM((NY, 2, 128, 128), F32),
            pltpu.VMEM((NY, 2, 128, 128), F32),
            pltpu.VMEM((NY, 128, 128), F32),
            pltpu.VMEM((512, 128), F32),
            pltpu.VMEM((2, NY, NX, 128, 128), BF),
            pltpu.VMEM((NY - 1, 128, 128), BF),
            pltpu.VMEM((512, 128), BF),
            pltpu.SemaphoreType.DMA((N_LINKS,)),
            pltpu.SemaphoreType.DMA((N_LINKS,)),
            pltpu.SemaphoreType.DMA((2,)),
            pltpu.SemaphoreType.DMA((NY,)),
            pltpu.SemaphoreType.DMA((4,)),
            pltpu.SemaphoreType.DMA((3,)),
        ],
        compiler_params=pltpu.CompilerParams(
            collective_id=0, has_side_effects=True, vmem_limit_bytes=60 * 1024 * 1024
        ),
    )(root_inv, panel, pattern.T, child_diag, owner)
    return pl.pallas_call(
        outputs,
        out_shape=(
            jax.ShapeDtypeStruct((1024, 128), F32),
            jax.ShapeDtypeStruct((512, 128), F32),
            jax.ShapeDtypeStruct((128, 512), BF),
        ),
        in_specs=[vmem] * 3,
        out_specs=(vmem,) * 3,
        compiler_params=pltpu.CompilerParams(vmem_limit_bytes=60 * 1024 * 1024),
    )(off, diag, own)


def solution(mesh):
    placed = (P("row", "col"), P(None, "col"), P(), P("row", "col"), P())
    return jax.shard_map(
        on_device,
        mesh=mesh,
        in_specs=placed,
        out_specs=(P("row", "col"), P("row", "col"), P("col", "row")),
        check_vma=False,
    )
```
